128 devices in a mesh: ctx: 32 (over x, z, y_lo), head: 4 (over y_hi, core).
Axes of the slice: x: 4, y: 4 (y_hi: 2, y_lo: 2; y = y_hi * 2 + y_lo), z: 4, core: 2. Of those that a mesh axis runs over, the one named last changes fastest.
Arguments:
- latent: bfloat16 [8192, 576], P('ctx'), may hold values from -8 to 8
- query: bfloat16 [8192, 12288], P('ctx', 'head'), may hold values from -300 to 300
- d_out: bfloat16 [8192, 8192], P('ctx', 'head'), may hold values from -6 to 6
- w_uk: bfloat16 [64, 128, 512], P('head'), may hold values from -0.5 to 0.5
- w_uv: bfloat16 [64, 128, 512], P('head'), may hold values from -0.25 to 0.25
- block_mask: int32 [32, 32], replicated, may hold values 0 or 1
- segments: int32 [8192], replicated, may hold values from 0 to 15, never falling along the last dimension, each value on 1 to 1536 neighbouring positions
Outputs:
- attended: bfloat16 [8192, 8192], P('ctx', 'head')
- d_query: bfloat16 [8192, 12288], P('ctx', 'head')
- d_latent: float32 [8192, 576], P('ctx')
- d_w_uk: float32 [64, 128, 512], P('head')
- d_w_uv: float32 [64, 128, 512], P('head')
The draws below stay inside these ranges and needn't reach their ends.
Inputs may be any that keep to these rules, and one draw needn't show every extreme that they name: block_mask[a, b] = 1 lets every token of block a read every earlier token of block b whatever their dialogues. `segments`: dialogue ids never fall along the sequence; each dialogue holds 1 to 1536 tokens and one holds exactly 1536.
All inputs are finite; a program needn't handle non-finite values.
Results may differ from the reference program's by a relative error of at most 0.012.
The reference program's roundings to bfloat16 on the way (of `q_nope`, `absorbed`, `q_full`, `probs_low`, `latent_out`, `d_latent_out`, `d_scores` and `d_absorbed`) count: a program that leaves them out, or rounds other values in their place, can miss the bound.
Values may be sent and summed in bfloat16 or wider, within the bound.
No kernel may reach another device: no remote copies, remote signals or barrier semaphores. Data moves between devices by JAX's collectives and lax.ppermute only.
A program may use at most 256 MiB of HBM per device.

```python
import math
import jax
import jax.numpy as jnp
import numpy as np
from jax import lax

TOK_DEV = 256
HEADS = 64
NOPE = 128
ROPE = 64
RANK = 512
VDIM = 128
SPAN = 2
LAT = 576
QW = 192
TOKENS = 8192
NSEG = 16
N_CTX = 32


def shared_rope(key):
    return jnp.clip(jax.random.normal(key, (TOKENS, ROPE), jnp.float32), -4.0, 4.0)


def draw_latent(key, part):
    key_rope = shared_rope(key)
    key = jax.random.fold_in(key, 3)
    key_values = jax.random.fold_in(key, 0)
    values = jnp.clip(jax.random.normal(key_values, (TOKENS, RANK), jnp.float32), -4.0, 4.0)
    return jnp.concatenate([values, key_rope], axis=1).astype(jnp.bfloat16)


def draw_query(key, part):
    key = jax.random.fold_in(key, 5)
    key_values = jax.random.fold_in(key, 0)
    whole_query = jnp.clip(jax.random.normal(key_values, (TOKENS, HEADS, QW), jnp.float32), -4.0, 4.0)
    return whole_query.reshape(TOKENS, HEADS * QW).astype(jnp.bfloat16)


def with_ends(array, stream_key, smallest, top_value):
    index_at = [jax.random.randint(jax.random.fold_in(stream_key, axis), (), 0, length) for axis, length in enumerate(array.shape)]
    main_axis = array.shape.index(max(array.shape))
    next_to = index_at[:main_axis] + [(index_at[main_axis] + 1) % array.shape[main_axis]] + index_at[main_axis + 1:]
    return array.at[tuple(index_at)].set(smallest).at[tuple(next_to)].set(top_value)


def steps_of(own_key, dims, cuts, least, high):
    gain, own = 1.0, jax.random.fold_in(own_key, 6)
    for dim, shards_of in cuts:
        draws = jnp.exp(jax.random.uniform(jax.random.fold_in(own, dim), (shards_of,), jnp.float32, least / len(cuts), high / len(cuts)))
        gain = gain * jnp.repeat(draws, dims[dim] // shards_of).reshape([-1 if axis == dim else 1 for axis in range(len(dims))])
    return gain


def split_up(count, total, most, lean):
    loads = [(1 << 20) // math.isqrt(standing ** lean) + 1 for standing in range(2, count + 1)]
    surplus, counts = total - most - (count - 1), [1] * (count - 1)
    while surplus > 0:
        movable = [i for i in range(count - 1) if counts[i] < most]
        pool, remaining = sum([loads[i] for i in movable]), surplus
        for i in movable:
            extra = min(most - counts[i], max(1, remaining * loads[i] // pool), surplus)
            counts[i] = counts[i] + extra
            surplus = surplus - extra
    return np.array([most] + counts)


def uneven(key, number_of, total, limit, lean):
    if number_of == 2:
        one = jax.random.randint(key, (), max(1, total - limit), min(limit, total - 1) + 1)
        return jnp.stack([one, total - one])
    sizes = jnp.asarray(split_up(number_of, total, limit, lean), jnp.int32)
    couples = (number_of - 1) // 2
    source_of, sink = sizes[1:1 + 2 * couples:2], sizes[2:2 + 2 * couples:2]
    room = jnp.minimum(source_of - 1, limit - sink)
    passed = jax.random.randint(jax.random.fold_in(key, 1), (couples,), 0, 1 << 20) % (room + 1)
    sizes = sizes.at[1:1 + 2 * couples:2].set(source_of - passed).at[2:2 + 2 * couples:2].set(sink + passed)
    return sizes[jax.random.permutation(jax.random.fold_in(key, 2), number_of)]


def noise(own_key, dims, scale, limit, shards=(), held_as=jnp.bfloat16):
    drawn = jax.random.normal(own_key, dims, jnp.float32) * scale
    if len(shards) > 0:
        drawn = steps_of(own_key, dims, shards, -0.22, 0.18) * drawn
    return jnp.clip(drawn, min=-limit, max=limit).astype(held_as)


def setup_inputs(seed: int = 0) -> dict:
    seeds = jax.random.split(jax.random.key(seed), 8)
    return {
        "latent": draw_latent(jax.random.fold_in(seeds[7], 71), 0),
        "query": draw_query(jax.random.fold_in(seeds[7], 71), 0),
        "d_out": noise(seeds[2], (TOKENS, HEADS * VDIM), 1.0, 6.0, ((0, 32), (1, 4))),
        "w_uk": noise(seeds[3], (HEADS, NOPE, RANK), NOPE ** -0.5, 0.5, ((0, 4),)),
        "w_uv": noise(seeds[4], (HEADS, VDIM, RANK), RANK ** -0.5, 0.25, ((0, 4),)),
        "block_mask": with_ends((jax.random.randint(seeds[5], (N_CTX, N_CTX), 0, 2) < 1).astype(jnp.int32), jax.random.fold_in(seeds[5], 1), 0, 1),
        "segments": jnp.searchsorted(jnp.cumsum(uneven(seeds[6], NSEG, TOKENS, 6 * TOK_DEV, 0)), jnp.arange(TOKENS), side="right").astype(jnp.int32),
    }


def rounded(values):
    return lax.optimization_barrier(values.astype(jnp.bfloat16))

def widen(values):
    return values.astype(jnp.float32)

def reference(latent, query, d_out, w_uk, w_uv, block_mask, segments):
    inv_root = 1.0 / math.sqrt(QW)
    queries = query.reshape(TOKENS, HEADS, QW)
    grads_all = d_out.reshape(TOKENS, HEADS, VDIM)
    padded = jnp.concatenate([jnp.zeros((SPAN * TOK_DEV, LAT), latent.dtype), latent], axis=0)
    seg_padded = jnp.concatenate([jnp.zeros((SPAN * TOK_DEV,), jnp.int32), segments.astype(jnp.int32)], axis=0)
    w_uk_wide = widen(w_uk)
    w_uv_wide = widen(w_uv)
    width = (SPAN + 1) * TOK_DEV
    offsets_q = jnp.arange(TOK_DEV, dtype=jnp.int32)
    offsets_k = jnp.arange(width, dtype=jnp.int32)

    def query_block(carried, block_id):
        d_keys_all, grad_uk, grad_uv = carried
        start = (block_id * TOK_DEV).astype(jnp.int32)
        q_here = lax.dynamic_slice_in_dim(queries, start, TOK_DEV, 0)
        q_nope = q_here[:, :, :NOPE]
        q_rope = q_here[:, :, NOPE:]
        absorbed = rounded(jnp.einsum('thn,hnr->thr', widen(q_nope), w_uk_wide))
        q_full = jnp.concatenate([absorbed, q_rope], axis=2)
        keys = lax.dynamic_slice_in_dim(padded, start, width, 0)
        content = keys[:, :RANK]
        seg_keys = lax.dynamic_slice_in_dim(seg_padded, start, width, 0)
        seg_query = lax.dynamic_slice_in_dim(segments.astype(jnp.int32), start, TOK_DEV, 0)
        key_block = block_id - SPAN + offsets_k // TOK_DEV
        granted = block_mask[block_id, jnp.maximum(key_block, 0)]
        q_pos = start + offsets_q
        k_pos = start - SPAN * TOK_DEV + offsets_k
        allowed = (key_block >= 0)[None, :] & (k_pos[None, :] <= q_pos[:, None]) & ((seg_query[:, None] == seg_keys[None, :]) | (granted == 1)[None, :])
        scores = jnp.einsum('thl,kl->htk', widen(q_full), widen(keys)) * inv_root
        scores = jnp.where(allowed[None], scores, -jnp.inf)
        row_max = lax.optimization_barrier(jnp.max(scores, axis=2, keepdims=True))
        weights = jnp.exp(scores - row_max)
        probs = weights / lax.optimization_barrier(jnp.sum(weights, axis=2, keepdims=True))
        probs_low = rounded(probs)
        latent_out = rounded(jnp.einsum('htk,kr->thr', widen(probs_low), widen(content)))
        attended = jnp.einsum('thr,hvr->thv', widen(latent_out), w_uv_wide).astype(jnp.bfloat16)
        grads = lax.dynamic_slice_in_dim(grads_all, start, TOK_DEV, 0)
        d_latent_out = rounded(jnp.einsum('thv,hvr->thr', widen(grads), w_uv_wide))
        grad_uv = grad_uv + jnp.einsum('thv,thr->hvr', widen(grads), widen(latent_out))
        d_probs = jnp.einsum('thr,kr->htk', widen(d_latent_out), widen(content))
        delta = lax.optimization_barrier(jnp.sum(probs * d_probs, axis=2, keepdims=True))
        d_scores = rounded(probs * (d_probs - delta) * inv_root)
        d_full = jnp.einsum('htk,kl->thl', widen(d_scores), widen(keys))
        d_absorbed = rounded(d_full[:, :, :RANK])
        d_nope = jnp.einsum('thr,hnr->thn', widen(d_absorbed), w_uk_wide)
        d_query = jnp.concatenate([d_nope, d_full[:, :, RANK:]], axis=2).astype(jnp.bfloat16)
        grad_uk = grad_uk + jnp.einsum('thn,thr->hnr', widen(q_nope), widen(d_absorbed))
        d_keys = jnp.einsum('htk,thl->kl', widen(d_scores), widen(q_full)) + jnp.pad(jnp.einsum('htk,thr->kr', widen(probs_low), widen(d_latent_out)), ((0, 0), (0, ROPE)))
        previous = lax.dynamic_slice_in_dim(d_keys_all, start, width, 0)
        d_keys_all = lax.dynamic_update_slice_in_dim(d_keys_all, previous + d_keys, start, 0)
        return ((d_keys_all, grad_uk, grad_uv), (attended.reshape(TOK_DEV, HEADS * VDIM), d_query.reshape(TOK_DEV, HEADS * QW)))
    initial = (jnp.zeros(((N_CTX + SPAN) * TOK_DEV, LAT), jnp.float32), jnp.zeros((HEADS, NOPE, RANK), jnp.float32), jnp.zeros((HEADS, VDIM, RANK), jnp.float32))
    finals, stacked = lax.scan(query_block, initial, jnp.arange(N_CTX, dtype=jnp.int32))
    d_keys_all, grad_uk, grad_uv = finals
    attended, d_query = stacked
    return (attended.reshape(TOKENS, HEADS * VDIM), d_query.reshape(TOKENS, HEADS * QW), d_keys_all[SPAN * TOK_DEV:], grad_uk, grad_uv)
```

```python
import functools
import math

import jax
import jax.numpy as jnp
from jax import lax
from jax.experimental import pallas as pl
from jax.experimental.pallas import tpu as pltpu
from jax.sharding import PartitionSpec as P

SPAN = 2
LOG2E = 1.4426950408889634
VMEM_LIMIT = 56 * 1024 * 1024


def shifted(block, axis, distance):
    devices = range(lax.axis_size(axis))
    route = [(i - distance, i) for i in devices if i - distance in devices]
    return lax.ppermute(block, axis, route)


def dot(a, b):
    return lax.dot_general(a, b, (((1,), (0,)), ((), ())), preferred_element_type=jnp.float32)


def dot_nt(a, b):
    return lax.dot_general(a, b, (((1,), (1,)), ((), ())), preferred_element_type=jnp.float32)


def prepare_kernel(query_ref, dout_ref, wuk_ref, wuv_ref, qfull_ref, dlo_ref, dout_t_ref, nope_t_ref):
    nope = wuk_ref.shape[1]
    value = wuv_ref.shape[1]
    width = query_ref.shape[1] // 2
    rank = wuk_ref.shape[2]
    query_t = query_ref[...].T
    dout_t = dout_ref[...].T
    for n in range(2):
        q_nope = query_t[n * width : n * width + nope]
        grads = dout_t[n * value : (n + 1) * value]
        nope_t_ref[n] = q_nope
        dout_t_ref[n] = grads
        qfull_ref[n, :rank] = dot(wuk_ref[n].T, q_nope).astype(jnp.bfloat16)
        qfull_ref[n, rank:] = query_t[n * width + nope : (n + 1) * width]
        dlo_ref[n] = dot(wuv_ref[n].T, grads).astype(jnp.bfloat16)


def prepare(query, d_out, w_uk, w_uv):
    toks = query.shape[0]
    heads, nope, rank = w_uk.shape
    value = w_uv.shape[1]
    width = query.shape[1] // heads
    lat = rank + width - nope
    shape = lambda rows: jax.ShapeDtypeStruct((heads, rows, toks), jnp.bfloat16)
    block = lambda rows: pl.BlockSpec((2, rows, toks), lambda s: (s, 0, 0))
    return pl.pallas_call(
        prepare_kernel,
        grid=(heads // 2,),
        in_specs=[
            pl.BlockSpec((toks, 2 * width), lambda s: (0, s)),
            pl.BlockSpec((toks, 2 * value), lambda s: (0, s)),
            pl.BlockSpec((2, nope, rank), lambda s: (s, 0, 0)),
            pl.BlockSpec((2, value, rank), lambda s: (s, 0, 0)),
        ],
        out_specs=[block(lat), block(rank), block(value), block(nope)],
        out_shape=[shape(lat), shape(rank), shape(value), shape(nope)],
        compiler_params=pltpu.CompilerParams(vmem_limit_bytes=VMEM_LIMIT),
        cost_estimate=pl.CostEstimate(
            flops=4 * heads * toks * nope * rank, bytes_accessed=16 * 2**20, transcendentals=0
        ),
        name="prepare",
    )(query, d_out, w_uk, w_uv)


def attend_kernel(
    inv_root,
    keys_ref,
    bias_ref,
    qfull_ref,
    dlo_ref,
    dout_t_ref,
    nope_t_ref,
    wuk_ref,
    wuv_ref,
    att_ref,
    dq_ref,
    guk_ref,
    guv_ref,
    dlat_ref,
    keys_t_ref,
):
    step = pl.program_id(0)
    rank = wuk_ref.shape[2]
    nope = wuk_ref.shape[1]
    value = wuv_ref.shape[1]
    width = dq_ref.shape[1] // 2

    @pl.when(step == 0)
    def _():
        keys_t_ref[...] = keys_ref[...].T
        dlat_ref[...] = jnp.zeros_like(dlat_ref)

    for n in range(2):
        qfull = qfull_ref[n]
        dlo = dlo_ref[n]
        scaled = dot(keys_ref[...], qfull) * (inv_root * LOG2E) + bias_ref[...]
        top = jnp.max(scaled, axis=0, keepdims=True)
        weights = jnp.exp2(scaled - top)
        probs = weights * (1.0 / jnp.sum(weights, axis=0, keepdims=True))
        probs_low = probs.astype(jnp.bfloat16)
        latent_out = dot(keys_t_ref[:rank], probs_low).astype(jnp.bfloat16)
        att_ref[:, n * value : (n + 1) * value] = dot(wuv_ref[n], latent_out).T.astype(jnp.bfloat16)
        guv_ref[n] = dot_nt(dout_t_ref[n], latent_out).astype(guv_ref.dtype)
        d_probs = dot(keys_ref[:, :rank], dlo)
        delta = jnp.sum(probs * d_probs, axis=0, keepdims=True)
        d_scores = (probs * (d_probs - delta) * inv_root).astype(jnp.bfloat16)
        d_full = dot(keys_t_ref[...], d_scores)
        d_absorbed = d_full[:rank].astype(jnp.bfloat16)
        d_nope = dot(wuk_ref[n], d_absorbed)
        guk_ref[n] = dot_nt(nope_t_ref[n], d_absorbed).astype(guk_ref.dtype)
        dq_ref[:, n * width : n * width + nope] = d_nope.T.astype(jnp.bfloat16)
        dq_ref[:, n * width + nope : (n + 1) * width] = d_full[rank:].T.astype(jnp.bfloat16)
        dlat_ref[:rank] += dot_nt(qfull[:rank], d_scores) + dot_nt(dlo, probs_low)
        dlat_ref[rank:] += dot_nt(qfull[rank:], d_scores)


def attend(keys, bias, qfull, dlo, dout_t, nope_t, w_uk, w_uv, inv_root):
    heads, nope, rank = w_uk.shape
    value = w_uv.shape[1]
    span, lat = keys.shape
    toks = qfull.shape[2]
    width = nope + lat - rank
    whole = lambda rows, cols: pl.BlockSpec((rows, cols), lambda s: (0, 0))
    pair = lambda rows, cols: pl.BlockSpec((2, rows, cols), lambda s: (s, 0, 0))
    out = jax.ShapeDtypeStruct
    return pl.pallas_call(
        functools.partial(attend_kernel, inv_root),
        grid=(heads // 2,),
        in_specs=[
            whole(span, lat),
            whole(span, toks),
            pair(lat, toks),
            pair(rank, toks),
            pair(value, toks),
            pair(nope, toks),
            pair(nope, rank),
            pair(value, rank),
        ],
        out_specs=[
            pl.BlockSpec((toks, 2 * value), lambda s: (0, s)),
            pl.BlockSpec((toks, 2 * width), lambda s: (0, s)),
            pair(nope, rank),
            pair(value, rank),
            whole(lat, span),
        ],
        out_shape=[
            out((toks, heads * value), jnp.bfloat16),
            out((toks, heads * width), jnp.bfloat16),
            out((heads, nope, rank), jnp.bfloat16),
            out((heads, value, rank), jnp.bfloat16),
            out((lat, span), jnp.float32),
        ],
        scratch_shapes=[pltpu.VMEM((lat, span), jnp.bfloat16)],
        compiler_params=pltpu.CompilerParams(vmem_limit_bytes=VMEM_LIMIT),
        cost_estimate=pl.CostEstimate(
            flops=heads * toks * (span * 4 * (rank + lat) + span * 2 * (rank + lat) + 8 * nope * rank),
            bytes_accessed=30 * 2**20,
            transcendentals=heads * toks * span,
        ),
        name="attend",
    )(keys, bias, qfull, dlo, dout_t, nope_t, w_uk, w_uv)


def summed_over_ctx(grads):
    rows, cols = grads.shape
    parts = lax.axis_size("ctx")
    pieces = lax.all_to_all(grads.reshape(parts, rows // parts, cols), "ctx", 0, 0, tiled=True)
    mine = jnp.sum(pieces.astype(jnp.float32), axis=0).astype(grads.dtype)
    sent = jnp.broadcast_to(mine[None], (parts,) + mine.shape)
    return lax.all_to_all(sent, "ctx", 0, 0, tiled=True).reshape(rows, cols)


def body(latent, query, d_out, w_uk, w_uv, block_mask, segments):
    toks, lat = latent.shape
    heads, nope, rank = w_uk.shape
    value = w_uv.shape[1]
    width = query.shape[1] // heads
    inv_root = 1.0 / math.sqrt(width)
    position = lax.axis_index("ctx")
    earlier = [shifted(latent, "ctx", distance) for distance in (2, 1)]
    qfull, dlo, dout_t, nope_t = prepare(query, d_out, w_uk, w_uv)

    offsets = jnp.arange(toks, dtype=jnp.int32)
    seg_query = lax.dynamic_slice_in_dim(segments, position * toks, toks)
    bias = []
    for distance in (2, 1, 0):
        block = position - distance
        clamped = jnp.maximum(block, 0)
        seg_key = lax.dynamic_slice_in_dim(segments, clamped * toks, toks)
        granted = block_mask[position, clamped]
        allowed = (
            (block >= 0)
            & (offsets[:, None] - distance * toks <= offsets[None, :])
            & ((seg_key[:, None] == seg_query[None, :]) | (granted == 1))
        )
        bias.append(jnp.where(allowed, 0.0, -jnp.inf).astype(jnp.float32))
    bias = jnp.concatenate(bias, axis=0)
    keys = jnp.concatenate(earlier + [latent], axis=0)
    attended, d_query, guk, guv, dlat_t = attend(
        keys, bias, qfull, dlo, dout_t, nope_t, w_uk, w_uv, inv_root
    )
    dlat = dlat_t.T
    returned = [
        shifted(dlat[part * toks : (part + 1) * toks].astype(jnp.bfloat16), "ctx", part - SPAN)
        for part in range(SPAN)
    ]
    own = dlat[SPAN * toks :] + (returned[0].astype(jnp.float32) + returned[1].astype(jnp.float32))
    d_latent = lax.psum(own, "head")
    grads = jnp.concatenate([guk.reshape(heads * nope, rank), guv.reshape(heads * value, rank)], axis=0)
    grads = summed_over_ctx(grads).astype(jnp.float32)
    d_w_uk = grads[: heads * nope].reshape(w_uk.shape)
    d_w_uv = grads[heads * nope :].reshape(w_uv.shape)
    return attended, d_query, d_latent, d_w_uk, d_w_uv


def solution(mesh):
    in_specs = (
        P("ctx", None),
        P("ctx", "head"),
        P("ctx", "head"),
        P("head", None, None),
        P("head", None, None),
        P(),
        P(),
    )
    out_specs = (
        P("ctx", "head"),
        P("ctx", "head"),
        P("ctx", None),
        P("head", None, None),
        P("head", None, None),
    )
    return jax.shard_map(body, mesh=mesh, in_specs=in_specs, out_specs=out_specs, check_vma=False)
```

```python
import functools
import math

import jax
import jax.numpy as jnp
from jax import lax
from jax.experimental import pallas as pl
from jax.experimental.pallas import tpu as pltpu
from jax.sharding import PartitionSpec as P

SPAN = 2
CHUNKS = 2
GROUP = 4
LOG2E = 1.4426950408889634
MIB = 2**20
LARGE = 56 * MIB
BRIEF = pl.CostEstimate(flops=2**20, bytes_accessed=2**20, transcendentals=0)


def shifted(block, axis, distance):
    devices = range(lax.axis_size(axis))
    route = [(i - distance, i) for i in devices if i - distance in devices]
    return lax.ppermute(block, axis, route)


def dot(a, b):
    return lax.dot_general(a, b, (((1,), (0,)), ((), ())), preferred_element_type=jnp.float32)


def dot_nt(a, b):
    return lax.dot_general(a, b, (((1,), (1,)), ((), ())), preferred_element_type=jnp.float32)


def prepare_kernel(query_ref, dout_ref, wuk_ref, wuv_ref, qfull_ref, dlo_ref, dout_t_ref, nope_t_ref):
    nope = wuk_ref.shape[1]
    value = wuv_ref.shape[1]
    width = query_ref.shape[1] // wuk_ref.shape[0]
    rank = wuk_ref.shape[2]
    query_t = query_ref[...].T
    dout_t = dout_ref[...].T
    for n in range(wuk_ref.shape[0]):
        q_nope = query_t[n * width : n * width + nope]
        grads = dout_t[n * value : (n + 1) * value]
        nope_t_ref[n] = q_nope
        dout_t_ref[n] = grads
        qfull_ref[n, :rank] = dot(wuk_ref[n].T, q_nope).astype(jnp.bfloat16)
        qfull_ref[n, rank:] = query_t[n * width + nope : (n + 1) * width]
        dlo_ref[n] = dot(wuv_ref[n].T, grads).astype(jnp.bfloat16)


def prepare(query, d_out, w_uk, w_uv):
    toks = query.shape[0]
    heads, nope, rank = w_uk.shape
    value = w_uv.shape[1]
    width = query.shape[1] // heads
    lat = rank + width - nope
    shape = lambda rows: jax.ShapeDtypeStruct((heads, rows, toks), jnp.bfloat16)
    block = lambda rows: pl.BlockSpec((GROUP, rows, toks), lambda s: (s, 0, 0))
    return pl.pallas_call(
        prepare_kernel,
        grid=(heads // GROUP,),
        in_specs=[
            pl.BlockSpec((toks, GROUP * width), lambda s: (0, s)),
            pl.BlockSpec((toks, GROUP * value), lambda s: (0, s)),
            pl.BlockSpec((GROUP, nope, rank), lambda s: (s, 0, 0)),
            pl.BlockSpec((GROUP, value, rank), lambda s: (s, 0, 0)),
        ],
        out_specs=[block(lat), block(rank), block(value), block(nope)],
        out_shape=[shape(lat), shape(rank), shape(value), shape(nope)],
        compiler_params=pltpu.CompilerParams(vmem_limit_bytes=LARGE),
        cost_estimate=pl.CostEstimate(
            flops=4 * heads * toks * nope * rank, bytes_accessed=16 * 2**20, transcendentals=0
        ),
        name="prepare",
    )(query, d_out, w_uk, w_uv)


def score_kernel(
    inv_root,
    block_refs,
    bias_ref,
    qfull_ref,
    dlo_ref,
    dout_t_ref,
    nope_t_ref,
    *rest,
):
    probs_ref, dscore_ref, lout_ref, dfull_ref, grad_ref, keys_ref, keys_t_ref = rest[-7:]
    rank = dlo_ref.shape[1]
    nope = nope_t_ref.shape[1]
    group = range(qfull_ref.shape[0])

    @pl.when(pl.program_id(0) == 0)
    def _():
        for n, block_ref in enumerate(block_refs):
            toks = block_ref.shape[1]
            keys_t_ref[:, n * toks : (n + 1) * toks] = block_ref[...]
            keys_ref[n * toks : (n + 1) * toks] = block_ref[...].T

    scores = [dot(keys_ref[...], qfull_ref[n]) for n in group]
    probs = []
    for n in group:
        scaled = scores[n] * (inv_root * LOG2E) + bias_ref[...]
        weights = jnp.exp2(scaled - jnp.max(scaled, axis=0, keepdims=True))
        probs.append(weights * (1.0 / jnp.sum(weights, axis=0, keepdims=True)))
        probs_ref[n] = probs[n].astype(jnp.bfloat16)
    d_probs = [dot(keys_ref[:, :rank], dlo_ref[n]) for n in group]
    for n in group:
        lout_ref[n] = dot(keys_t_ref[:rank], probs_ref[n]).astype(jnp.bfloat16)
    for n in group:
        delta = jnp.sum(probs[n] * d_probs[n], axis=0, keepdims=True)
        dscore_ref[n] = (probs[n] * (d_probs[n] - delta) * inv_root).astype(jnp.bfloat16)
    for n in group:
        grad_ref[n, nope:] = dot_nt(dout_t_ref[n], lout_ref[n]).astype(jnp.bfloat16)
    for n in group:
        dfull_ref[n] = dot(keys_t_ref[...], dscore_ref[n]).astype(jnp.bfloat16)
    for n in group:
        grad_ref[n, :nope] = dot_nt(nope_t_ref[n], dfull_ref[n, :rank]).astype(jnp.bfloat16)


def score(blocks, bias, qfull, dlo, dout_t, nope_t, inv_root, start, count, carried, after):
    heads, lat, toks = qfull.shape
    span = bias.shape[0]
    rank = dlo.shape[1]
    value, nope = dout_t.shape[1], nope_t.shape[1]
    base = start // GROUP
    whole = lambda rows, cols: pl.BlockSpec((rows, cols), lambda s: (0, 0))
    heads_of = lambda rows: pl.BlockSpec((GROUP, rows, toks), lambda s: (s + base, 0, 0))
    out = lambda rows: jax.ShapeDtypeStruct((heads, rows, toks), jnp.bfloat16)
    return pl.pallas_call(
        functools.partial(score_kernel, inv_root),
        grid=(count // GROUP,),
        in_specs=[
            [whole(lat, toks)] * len(blocks),
            whole(span, toks),
            heads_of(lat),
            heads_of(rank),
            heads_of(value),
            heads_of(nope),
        ]
        + [pl.BlockSpec(memory_space=pl.ANY)] * (len(carried) + len(after)),
        out_specs=[
            heads_of(span),
            heads_of(span),
            heads_of(rank),
            heads_of(lat),
            pl.BlockSpec((GROUP, nope + value, rank), lambda s: (s, 0, 0)),
        ],
        out_shape=[
            out(span),
            out(span),
            out(rank),
            out(lat),
            jax.ShapeDtypeStruct((count, nope + value, rank), jnp.bfloat16),
        ],
        input_output_aliases={5 + len(blocks) + n: n for n in range(len(carried))},
        scratch_shapes=[pltpu.VMEM((span, lat), jnp.bfloat16), pltpu.VMEM((lat, span), jnp.bfloat16)],
        compiler_params=pltpu.CompilerParams(vmem_limit_bytes=LARGE),
        cost_estimate=pl.CostEstimate(
            flops=8 * count * toks * span * (rank + lat),
            bytes_accessed=3 * count * 2**20,
            transcendentals=count * toks * span,
        ),
        name="score",
    )(blocks, bias, qfull, dlo, dout_t, nope_t, *carried, *after)


def key_kernel(last, core_ref, qfull_ref, dlo_ref, probs_ref, dscore_ref, *rest):
    total_ref = rest[-1]
    rank = dlo_ref.shape[1]
    step = pl.program_id(0)

    @pl.when(step == 0)
    def _():
        total_ref[...] = rest[0][...] if last else jnp.zeros_like(total_ref)

    content = 0.0
    rope = 0.0
    for n in range(qfull_ref.shape[0]):
        content += dot_nt(qfull_ref[n, :rank], dscore_ref[n]) + dot_nt(dlo_ref[n], probs_ref[n])
        rope += dot_nt(qfull_ref[n, rank:], dscore_ref[n])
    total_ref[:rank] += content
    total_ref[rank:] += rope

    if last:
        keep_ref, send_ref = rest[-3:-1]
        rows = keep_ref.shape[0]

        @pl.when(step == pl.num_programs(0) - 1)
        def _():
            keep_ref[...] = total_ref[pl.ds(pl.multiple_of(core_ref[0] * rows, rows), rows)]
            send_ref[...] = total_ref[pl.ds(pl.multiple_of((1 - core_ref[0]) * rows, rows), rows)]


def key_gradient(core, qfull, dlo, probs, dscore, start, count, last, carried, after):
    lat, toks = qfull.shape[1:]
    rank = dlo.shape[1]
    span = probs.shape[1]
    base = start // GROUP
    heads_of = lambda rows: pl.BlockSpec((GROUP, rows, toks), lambda s: (s + base, 0, 0))
    whole = lambda rows: pl.BlockSpec((rows, span), lambda s: (0, 0))
    out = lambda rows: jax.ShapeDtypeStruct((rows, span), jnp.float32)
    outputs = [lat // 2, lat // 2] if last else [lat]
    return pl.pallas_call(
        functools.partial(key_kernel, last),
        grid=(count // GROUP,),
        in_specs=[pl.BlockSpec(memory_space=pltpu.SMEM)]
        + [heads_of(lat), heads_of(rank), heads_of(span), heads_of(span)]
        + [whole(lat)] * len(carried)
        + [pl.BlockSpec(memory_space=pl.ANY)] * len(after),
        out_specs=[whole(rows) for rows in outputs],
        out_shape=[out(rows) for rows in outputs],
        scratch_shapes=[pltpu.VMEM((lat, span), jnp.float32)] if last else [],
        compiler_params=pltpu.CompilerParams(vmem_limit_bytes=LARGE),
        cost_estimate=BRIEF,
        name="key_gradient",
    )(core, qfull, dlo, probs, dscore, *carried, *after)


def split_kernel(keep_ref, got_ref, own_ref, *part_refs):
    toks = own_ref.shape[1]
    for part, part_ref in enumerate(part_refs):
        span = slice(part * toks, (part + 1) * toks)
        total = keep_ref[:, span] + got_ref[:, span]
        part_ref[...] = total.astype(part_ref.dtype)
        if part == len(part_refs) - 1:
            own_ref[...] = total


def split(keep, got, toks):
    rows, span = keep.shape
    out = lambda dtype: jax.ShapeDtypeStruct((rows, toks), dtype)
    return pl.pallas_call(
        split_kernel,
        out_shape=[out(jnp.float32)] + [out(jnp.bfloat16)] * (span // toks),
        compiler_params=pltpu.CompilerParams(vmem_limit_bytes=12 * MIB),
        cost_estimate=BRIEF,
        name="split",
    )(keep, got)


def merge_kernel(own_ref, *rest):
    total = own_ref[...]
    for part_ref in rest[:-2]:
        total += part_ref[...].astype(jnp.float32)
    rest[-1][...] = total


def merge(own, parts, after):
    whole = pl.BlockSpec(memory_space=pltpu.VMEM)
    return pl.pallas_call(
        merge_kernel,
        in_specs=[whole] * (1 + len(parts)) + [pl.BlockSpec(memory_space=pl.ANY)],
        out_specs=whole,
        out_shape=jax.ShapeDtypeStruct(own.shape, own.dtype),
        compiler_params=pltpu.CompilerParams(vmem_limit_bytes=12 * MIB),
        cost_estimate=BRIEF,
        name="merge",
    )(own, *parts, after)


def assemble_kernel(core_ref, mine_ref, other_ref, out_ref):
    rows = mine_ref.shape[0]
    core = core_ref[0]
    out_ref[pl.ds(pl.multiple_of(core * rows, rows), rows)] = mine_ref[...]
    out_ref[pl.ds(pl.multiple_of((1 - core) * rows, rows), rows)] = other_ref[...]


def assemble(core, mine, other):
    rows, toks = mine.shape
    whole = pl.BlockSpec(memory_space=pltpu.VMEM)
    return pl.pallas_call(
        assemble_kernel,
        in_specs=[pl.BlockSpec(memory_space=pltpu.SMEM), whole, whole],
        out_specs=whole,
        out_shape=jax.ShapeDtypeStruct((2 * rows, toks), jnp.float32),
        compiler_params=pltpu.CompilerParams(vmem_limit_bytes=12 * MIB),
        cost_estimate=BRIEF,
        name="assemble",
    )(core, mine, other)


def project_kernel(lout_ref, dfull_ref, wuk_ref, wuv_ref, att_ref, dq_ref):
    group = range(lout_ref.shape[0])
    rank = lout_ref.shape[1]
    value = wuv_ref.shape[1]
    width = dq_ref.shape[1] // len(group)
    for n in group:
        attended = dot(wuv_ref[n], lout_ref[n]).astype(jnp.bfloat16)
        att_ref[:, n * value : (n + 1) * value] = attended.T
        d_nope = dot(wuk_ref[n], dfull_ref[n, :rank]).astype(jnp.bfloat16)
        dq_ref[:, n * width : (n + 1) * width] = jnp.concatenate([d_nope, dfull_ref[n, rank:]], axis=0).T


def project(lout, dfull, w_uk, w_uv):
    heads, lat, toks = dfull.shape
    nope, rank = w_uk.shape[1:]
    value = w_uv.shape[1]
    width = nope + lat - rank
    heads_of = lambda rows, cols: pl.BlockSpec((GROUP, rows, cols), lambda s: (s, 0, 0))
    out = lambda cols: jax.ShapeDtypeStruct((toks, heads * cols), jnp.bfloat16)
    return pl.pallas_call(
        project_kernel,
        grid=(heads // GROUP,),
        in_specs=[heads_of(rank, toks), heads_of(lat, toks), heads_of(nope, rank), heads_of(value, rank)],
        out_specs=[
            pl.BlockSpec((toks, GROUP * value), lambda s: (0, s)),
            pl.BlockSpec((toks, GROUP * width), lambda s: (0, s)),
        ],
        out_shape=[out(value), out(width)],
        compiler_params=pltpu.CompilerParams(vmem_limit_bytes=LARGE),
        cost_estimate=BRIEF,
        name="project",
    )(lout, dfull, w_uk, w_uv)


def add_kernel(*refs):
    *piece_refs, _, _, out_ref = refs
    for chunk, piece_ref in enumerate(piece_refs):
        total = jnp.sum(piece_ref[...].astype(jnp.float32), axis=0).astype(out_ref.dtype)
        out_ref[:, chunk] = jnp.broadcast_to(total[None], piece_ref.shape)


def add_pieces(pieces, after):
    parts, rows, cols = pieces[0].shape
    tall = 16
    return pl.pallas_call(
        add_kernel,
        grid=(rows // tall,),
        in_specs=[pl.BlockSpec((parts, tall, cols), lambda s: (0, s, 0))] * len(pieces)
        + [pl.BlockSpec(memory_space=pl.ANY)] * len(after),
        out_specs=pl.BlockSpec((parts, len(pieces), tall, cols), lambda s: (0, 0, s, 0)),
        out_shape=jax.ShapeDtypeStruct((parts, len(pieces), rows, cols), jnp.bfloat16),
        compiler_params=pltpu.CompilerParams(vmem_limit_bytes=14 * MIB),
        cost_estimate=pl.CostEstimate(flops=2**21, bytes_accessed=8 * 2**20, transcendentals=0),
        name="add_pieces",
    )(*pieces, *after)


def widen_kernel(sums_ref, uk_ref, uv_ref):
    uk_ref[...] = sums_ref[:, 0, :, 0].astype(jnp.float32)
    uv_ref[...] = sums_ref[:, 1, :, 0].astype(jnp.float32)


def widen(sums, heads):
    parts, chunks, rows, cols = sums.shape
    per_chunk = heads // chunks
    half = parts // per_chunk // 2
    view = sums.reshape(per_chunk, 2, half, chunks, rows, cols)
    step = 2
    out = jax.ShapeDtypeStruct((heads, half, rows, cols), jnp.float32)
    place = lambda c, s: (c * (per_chunk // step) + s, 0, 0, 0)
    uk, uv = pl.pallas_call(
        widen_kernel,
        grid=(chunks, per_chunk // step),
        in_specs=[pl.BlockSpec((step, 2, half, 1, rows, cols), lambda c, s: (s, 0, 0, c, 0, 0))],
        out_specs=[pl.BlockSpec((step, half, rows, cols), place)] * 2,
        out_shape=[out, out],
        compiler_params=pltpu.CompilerParams(vmem_limit_bytes=14 * MIB),
        cost_estimate=pl.CostEstimate(flops=2**21, bytes_accessed=12 * 2**20, transcendentals=0),
        name="widen",
    )(view)
    return uk.reshape(heads, half * rows, cols), uv.reshape(heads, half * rows, cols)


def scattered(grads):
    parts = lax.axis_size("ctx")
    return lax.all_to_all(grads.reshape(parts, -1, grads.shape[-1]), "ctx", 0, 0, tiled=True)


def swap_core(block):
    return lax.ppermute(block, "head", [(0, 1), (1, 0), (2, 3), (3, 2)])


def returned(block, distance, across):
    blocks, heads = lax.axis_size("ctx"), lax.axis_size("head")
    route = [
        (c * heads + h, (c - distance) * heads + (h ^ 2 if across else h))
        for c in range(distance, blocks)
        for h in range(heads)
    ]
    return lax.ppermute(block, ("ctx", "head"), route)


def latent_gradient(core, keep, send, toks, after):
    own, *parts = split(keep, swap_core(send), toks)
    arrived = [returned(parts[SPAN], 0, True)]
    for distance in range(1, SPAN + 1):
        for across in (False, True):
            arrived.append(returned(parts[SPAN - distance], distance, across))
    mine = merge(own, arrived, after)
    return assemble(core, mine, swap_core(mine))


def body(latent, query, d_out, w_uk, w_uv, block_mask, segments):
    toks, lat = latent.shape
    heads, nope, rank = w_uk.shape
    width = query.shape[1] // heads
    inv_root = 1.0 / math.sqrt(width)
    position = lax.axis_index("ctx")
    latent_t = latent.T
    blocks = [shifted(latent_t, "ctx", distance) for distance in (2, 1)] + [latent_t]
    qfull, dlo, dout_t, nope_t = prepare(query, d_out, w_uk, w_uv)

    offsets = jnp.arange(toks, dtype=jnp.int32)
    seg_query = lax.dynamic_slice_in_dim(segments, position * toks, toks)
    bias = []
    for distance in (2, 1, 0):
        block = position - distance
        clamped = jnp.maximum(block, 0)
        seg_key = lax.dynamic_slice_in_dim(segments, clamped * toks, toks)
        granted = block_mask[position, clamped]
        allowed = (
            (block >= 0)
            & (offsets[:, None] - distance * toks <= offsets[None, :])
            & ((seg_key[:, None] == seg_query[None, :]) | (granted == 1))
        )
        bias.append(jnp.where(allowed, 0.0, -jnp.inf).astype(jnp.float32))
    bias = jnp.concatenate(bias, axis=0)
    core = (lax.axis_index("head") % 2).astype(jnp.int32).reshape(1)
    carried = []
    pieces = []
    dlat_t = []
    count = heads // CHUNKS
    for start in range(0, heads, count):
        *carried, grads = score(
            blocks, bias, qfull, dlo, dout_t, nope_t, inv_root, start, count, carried, dlat_t
        )
        pieces.append(scattered(grads))
        probs, dscore, lout, dfull = carried
        last = start + count == heads
        dlat_t = key_gradient(core, qfull, dlo, probs, dscore, start, count, last, dlat_t, pieces[:-1])
    attended, d_query = project(lout, dfull, w_uk, w_uv)
    d_latent_t = latent_gradient(core, *dlat_t, toks, attended)
    sums = add_pieces(pieces, (d_latent_t, attended))
    sums = lax.all_to_all(sums, "ctx", 0, 0, tiled=True)
    d_w_uk, d_w_uv = widen(sums, heads)
    return attended, d_query, d_latent_t.T, d_w_uk, d_w_uv


def solution(mesh):
    in_specs = (
        P("ctx", None),
        P("ctx", "head"),
        P("ctx", "head"),
        P("head", None, None),
        P("head", None, None),
        P(),
        P(),
    )
    out_specs = (
        P("ctx", "head"),
        P("ctx", "head"),
        P("ctx", None),
        P("head", None, None),
        P("head", None, None),
    )
    return jax.shard_map(body, mesh=mesh, in_specs=in_specs, out_specs=out_specs, check_vma=False)
```

```python
import functools
import math

import jax
import jax.numpy as jnp
from jax import lax
from jax.experimental import pallas as pl
from jax.experimental.pallas import tpu as pltpu
from jax.sharding import PartitionSpec as P

SPAN = 2
CHUNKS = 2
HOPS = (0, 1, -1, 2)
GROUP = 4
LOG2E = 1.4426950408889634
MIB = 2**20
LARGE = 56 * MIB
BRIEF = pl.CostEstimate(flops=2**20, bytes_accessed=2**20, transcendentals=0)


def shifted(block, axis, distance):
    devices = range(lax.axis_size(axis))
    route = [(i - distance, i) for i in devices if i - distance in devices]
    return lax.ppermute(block, axis, route)


def dot(a, b):
    return lax.dot_general(a, b, (((1,), (0,)), ((), ())), preferred_element_type=jnp.float32)


def dot_nt(a, b):
    return lax.dot_general(a, b, (((1,), (1,)), ((), ())), preferred_element_type=jnp.float32)


def prepare_kernel(query_ref, dout_ref, wuk_ref, wuv_ref, qfull_ref, dlo_ref, dout_t_ref, nope_t_ref):
    nope = wuk_ref.shape[1]
    value = wuv_ref.shape[1]
    width = query_ref.shape[1] // wuk_ref.shape[0]
    rank = wuk_ref.shape[2]
    query_t = query_ref[...].T
    dout_t = dout_ref[...].T
    for n in range(wuk_ref.shape[0]):
        q_nope = query_t[n * width : n * width + nope]
        grads = dout_t[n * value : (n + 1) * value]
        nope_t_ref[n] = q_nope
        dout_t_ref[n] = grads
        qfull_ref[n, :rank] = dot(wuk_ref[n].T, q_nope).astype(jnp.bfloat16)
        qfull_ref[n, rank:] = query_t[n * width + nope : (n + 1) * width]
        dlo_ref[n] = dot(wuv_ref[n].T, grads).astype(jnp.bfloat16)


def prepare(query, d_out, w_uk, w_uv):
    toks = query.shape[0]
    heads, nope, rank = w_uk.shape
    value = w_uv.shape[1]
    width = query.shape[1] // heads
    lat = rank + width - nope
    shape = lambda rows: jax.ShapeDtypeStruct((heads, rows, toks), jnp.bfloat16)
    block = lambda rows: pl.BlockSpec((GROUP, rows, toks), lambda s: (s, 0, 0))
    return pl.pallas_call(
        prepare_kernel,
        grid=(heads // GROUP,),
        in_specs=[
            pl.BlockSpec((toks, GROUP * width), lambda s: (0, s)),
            pl.BlockSpec((toks, GROUP * value), lambda s: (0, s)),
            pl.BlockSpec((GROUP, nope, rank), lambda s: (s, 0, 0)),
            pl.BlockSpec((GROUP, value, rank), lambda s: (s, 0, 0)),
        ],
        out_specs=[block(lat), block(rank), block(value), block(nope)],
        out_shape=[shape(lat), shape(rank), shape(value), shape(nope)],
        compiler_params=pltpu.CompilerParams(vmem_limit_bytes=LARGE),
        cost_estimate=pl.CostEstimate(
            flops=4 * heads * toks * nope * rank, bytes_accessed=16 * 2**20, transcendentals=0
        ),
        name="prepare",
    )(query, d_out, w_uk, w_uv)


def score_kernel(
    inv_root,
    which,
    place_ref,
    mask_ref,
    segments_ref,
    block_refs,
    qfull_ref,
    dlo_ref,
    dout_t_ref,
    nope_t_ref,
    *rest,
):
    probs_ref, dscore_ref, lout_ref, dfull_ref, *slab_refs, grad_ref, keys_ref, keys_t_ref, bias_ref = rest[-12:]
    rank = dlo_ref.shape[1]
    group = range(qfull_ref.shape[0])
    step = pl.program_id(0)

    @pl.when(step == 0)
    def _():
        for n, block_ref in enumerate(block_refs):
            toks = block_ref.shape[1]
            keys_t_ref[:, n * toks : (n + 1) * toks] = block_ref[...]
            keys_ref[n * toks : (n + 1) * toks] = block_ref[...].T
        position = place_ref[0]
        seg_query = segments_ref[pl.ds(position, 1)].astype(jnp.float32)
        for n in range(len(block_refs)):
            distance = len(block_refs) - 1 - n
            block = jnp.maximum(position - distance, 0)
            seg_row = segments_ref[pl.ds(block, 1)].astype(jnp.float32)
            seg_key = jnp.broadcast_to(seg_row, (toks, toks)).T
            granted = jnp.broadcast_to(mask_ref[position, block], (toks, toks)) == 1
            allowed = (seg_key == seg_query) | granted
            if distance == 0:
                key, query = (lax.broadcasted_iota(jnp.int32, (toks, toks), axis) for axis in (0, 1))
                allowed &= key <= query
            else:
                allowed &= jnp.broadcast_to(position, (toks, toks)) >= distance
            bias_ref[n * toks : (n + 1) * toks] = jnp.where(allowed, 0.0, -jnp.inf)

    scores = [dot(keys_ref[...], qfull_ref[n]) for n in group]
    probs = []
    for n in group:
        scaled = scores[n] * (inv_root * LOG2E) + bias_ref[...]
        weights = jnp.exp2(scaled - jnp.max(scaled, axis=0, keepdims=True))
        probs.append(weights * (1.0 / jnp.sum(weights, axis=0, keepdims=True)))
        probs_ref[n] = probs[n].astype(jnp.bfloat16)
    d_probs = [dot(keys_ref[:, :rank], dlo_ref[n]) for n in group]
    for n in group:
        lout_ref[n] = dot(keys_t_ref[:rank], probs_ref[n]).astype(jnp.bfloat16)
    for n in group:
        delta = jnp.sum(probs[n] * d_probs[n], axis=0, keepdims=True)
        dscore_ref[n] = (probs[n] * (d_probs[n] - delta) * inv_root).astype(jnp.bfloat16)
    def slab(n):
        return (step * (len(group) // 2) + n // 2 + 4 - place_ref[which]) % 4

    for n in group:
        grad_ref[slab(n), n % 2, 1] = dot_nt(dout_t_ref[n], lout_ref[n]).astype(jnp.bfloat16)
    for n in group:
        dfull_ref[n] = dot(keys_t_ref[...], dscore_ref[n]).astype(jnp.bfloat16)
    for n in group:
        grad_ref[slab(n), n % 2, 0] = dot_nt(nope_t_ref[n], dfull_ref[n, :rank]).astype(jnp.bfloat16)

    @pl.when(step == pl.num_programs(0) - 1)
    def _():
        for hop, slab_ref in zip(HOPS, slab_refs):
            slab_ref[...] = grad_ref[hop % 4].reshape(slab_ref.shape)


def score(which, place, block_mask, segments, blocks, qfull, dlo, dout_t, nope_t, inv_root, start, count, carried):
    heads, lat, toks = qfull.shape
    span = len(blocks) * toks
    rank = dlo.shape[1]
    value, nope = dout_t.shape[1], nope_t.shape[1]
    base = start // GROUP
    whole = lambda rows, cols: pl.BlockSpec((rows, cols), lambda s: (0, 0))
    heads_of = lambda rows: pl.BlockSpec((GROUP, rows, toks), lambda s: (s + base, 0, 0))
    out = lambda rows: jax.ShapeDtypeStruct((heads, rows, toks), jnp.bfloat16)
    return pl.pallas_call(
        functools.partial(score_kernel, inv_root, which),
        grid=(count // GROUP,),
        in_specs=[
            pl.BlockSpec(memory_space=pltpu.SMEM),
            pl.BlockSpec(memory_space=pltpu.SMEM),
            whole(*segments.shape),
            [whole(lat, toks)] * len(blocks),
            heads_of(lat),
            heads_of(rank),
            heads_of(value),
            heads_of(nope),
        ]
        + [pl.BlockSpec(memory_space=pl.ANY)] * len(carried),
        out_specs=[
            heads_of(span),
            heads_of(span),
            heads_of(rank),
            heads_of(lat),
        ]
        + [whole(4 * nope, rank)] * len(HOPS),
        out_shape=[
            out(span),
            out(span),
            out(rank),
            out(lat),
        ]
        + [jax.ShapeDtypeStruct((4 * nope, rank), jnp.bfloat16)] * len(HOPS),
        input_output_aliases={7 + len(blocks) + n: n for n in range(len(carried))},
        scratch_shapes=[
            pltpu.VMEM((4, 2, 2, nope, rank), jnp.bfloat16),
            pltpu.VMEM((span, lat), jnp.bfloat16),
            pltpu.VMEM((lat, span), jnp.bfloat16),
            pltpu.VMEM((span, toks), jnp.float32),
        ],
        compiler_params=pltpu.CompilerParams(vmem_limit_bytes=LARGE),
        cost_estimate=pl.CostEstimate(
            flops=8 * count * toks * span * (rank + lat),
            bytes_accessed=3 * count * 2**20,
            transcendentals=count * toks * span,
        ),
        name="score",
    )(place, block_mask, segments, blocks, qfull, dlo, dout_t, nope_t, *carried)


def key_kernel(qfull_ref, dlo_ref, probs_ref, dscore_ref, _, total_ref):
    rank = dlo_ref.shape[1]

    @pl.when(pl.program_id(0) == 0)
    def _():
        total_ref[...] = jnp.zeros_like(total_ref)

    content = 0.0
    rope = 0.0
    for n in range(qfull_ref.shape[0]):
        content += dot_nt(qfull_ref[n, :rank], dscore_ref[n]) + dot_nt(dlo_ref[n], probs_ref[n])
        rope += dot_nt(qfull_ref[n, rank:], dscore_ref[n])
    total_ref[:rank] += content
    total_ref[rank:] += rope


def key_gradient(qfull, dlo, probs, dscore, after):
    heads, lat, toks = qfull.shape
    rank = dlo.shape[1]
    span = probs.shape[1]
    heads_of = lambda rows: pl.BlockSpec((GROUP, rows, toks), lambda s: (s, 0, 0))
    return pl.pallas_call(
        key_kernel,
        grid=(heads // GROUP,),
        in_specs=[heads_of(lat), heads_of(rank), heads_of(span), heads_of(span)]
        + [pl.BlockSpec(memory_space=pl.ANY)],
        out_specs=pl.BlockSpec((lat, span), lambda s: (0, 0)),
        out_shape=jax.ShapeDtypeStruct((lat, span), jnp.float32),
        compiler_params=pltpu.CompilerParams(vmem_limit_bytes=LARGE),
        cost_estimate=pl.CostEstimate(
            flops=4 * heads * toks * span * (rank + lat), bytes_accessed=24 * MIB, transcendentals=0
        ),
        name="key_gradient",
    )(qfull, dlo, probs, dscore, after)


def split_kernel(keep_ref, got_ref, own_ref, *part_refs):
    toks = own_ref.shape[1]
    for part, part_ref in enumerate(part_refs + (own_ref,)):
        span = slice(part * toks, (part + 1) * toks)
        part_ref[...] = (keep_ref[:, span] + got_ref[:, span]).astype(part_ref.dtype)


def split(keep, got, toks):
    rows, span = keep.shape
    out = lambda dtype: jax.ShapeDtypeStruct((rows, toks), dtype)
    return pl.pallas_call(
        split_kernel,
        out_shape=[out(jnp.float32)] + [out(jnp.bfloat16)] * SPAN,
        compiler_params=pltpu.CompilerParams(vmem_limit_bytes=12 * MIB),
        cost_estimate=BRIEF,
        name="split",
    )(keep, got)


def merge_kernel(own_ref, *rest):
    *part_refs, out_ref = rest
    total = own_ref[...]
    for part_ref in part_refs:
        total += part_ref[...].astype(jnp.float32)
    out_ref[...] = total.astype(out_ref.dtype)


def merge(own, parts):
    return pl.pallas_call(
        merge_kernel,
        out_shape=jax.ShapeDtypeStruct(own.shape, jnp.bfloat16),
        compiler_params=pltpu.CompilerParams(vmem_limit_bytes=12 * MIB),
        cost_estimate=BRIEF,
        name="merge",
    )(own, *parts)


def finish_kernel(own_ref, far_ref, out_ref):
    out_ref[...] = own_ref[...].astype(jnp.float32) + far_ref[...].astype(jnp.float32)


def finish(own, far):
    return pl.pallas_call(
        finish_kernel,
        out_shape=jax.ShapeDtypeStruct(own.shape, jnp.float32),
        compiler_params=pltpu.CompilerParams(vmem_limit_bytes=12 * MIB),
        cost_estimate=BRIEF,
        name="finish",
    )(own, far)


def assemble_kernel(core_ref, mine_ref, other_ref, out_ref):
    rows = mine_ref.shape[0]
    core = core_ref[0]
    out_ref[pl.ds(pl.multiple_of(core * rows, rows), rows)] = mine_ref[...]
    out_ref[pl.ds(pl.multiple_of((1 - core) * rows, rows), rows)] = other_ref[...]


def assemble(core, mine, other):
    rows, toks = mine.shape
    whole = pl.BlockSpec(memory_space=pltpu.VMEM)
    return pl.pallas_call(
        assemble_kernel,
        in_specs=[pl.BlockSpec(memory_space=pltpu.SMEM), whole, whole],
        out_specs=whole,
        out_shape=jax.ShapeDtypeStruct((2 * rows, toks), jnp.float32),
        compiler_params=pltpu.CompilerParams(vmem_limit_bytes=12 * MIB),
        cost_estimate=BRIEF,
        name="assemble",
    )(core, mine, other)


def project_kernel(lout_ref, dfull_ref, wuk_ref, wuv_ref, _, att_ref, dq_ref):
    group = range(lout_ref.shape[0])
    rank = lout_ref.shape[1]
    value = wuv_ref.shape[1]
    width = dq_ref.shape[1] // len(group)
    for n in group:
        attended = dot(wuv_ref[n], lout_ref[n]).astype(jnp.bfloat16)
        att_ref[:, n * value : (n + 1) * value] = attended.T
        d_nope = dot(wuk_ref[n], dfull_ref[n, :rank]).astype(jnp.bfloat16)
        dq_ref[:, n * width : (n + 1) * width] = jnp.concatenate([d_nope, dfull_ref[n, rank:]], axis=0).T


def project(lout, dfull, w_uk, w_uv, after):
    heads, lat, toks = dfull.shape
    nope, rank = w_uk.shape[1:]
    value = w_uv.shape[1]
    width = nope + lat - rank
    heads_of = lambda rows, cols: pl.BlockSpec((GROUP, rows, cols), lambda s: (s, 0, 0))
    out = lambda cols: jax.ShapeDtypeStruct((toks, heads * cols), jnp.bfloat16)
    return pl.pallas_call(
        project_kernel,
        grid=(heads // GROUP,),
        in_specs=[heads_of(rank, toks), heads_of(lat, toks), heads_of(nope, rank), heads_of(value, rank)]
        + [pl.BlockSpec(memory_space=pl.ANY)],
        out_specs=[
            pl.BlockSpec((toks, GROUP * value), lambda s: (0, s)),
            pl.BlockSpec((toks, GROUP * width), lambda s: (0, s)),
        ],
        out_shape=[out(value), out(width)],
        compiler_params=pltpu.CompilerParams(vmem_limit_bytes=16 * MIB),
        cost_estimate=BRIEF,
        name="project",
    )(lout, dfull, w_uk, w_uv, after)


def reduce_kernel(which, place_ref, *refs):
    *slab_refs, _, own_ref, up_ref, down_ref, far_ref = refs
    rows = own_ref.shape[0]
    for hop, out_ref in zip(HOPS, (own_ref, up_ref, down_ref, far_ref)):
        span = pl.ds(pl.multiple_of(((place_ref[which] + hop + 4) % 4) * rows, rows), rows)
        total = 0.0
        for slab_ref in slab_refs:
            total += slab_ref[span].astype(jnp.float32)
        out_ref[...] = total.astype(out_ref.dtype)


def reduced(which, place, slabs, after):
    whole = pl.BlockSpec(memory_space=pltpu.VMEM)
    rows, cols = slabs[0].shape
    return pl.pallas_call(
        functools.partial(reduce_kernel, which),
        in_specs=[pl.BlockSpec(memory_space=pltpu.SMEM)]
        + [whole] * len(slabs)
        + [pl.BlockSpec(memory_space=pl.ANY)],
        out_specs=[whole] * 4,
        out_shape=[jax.ShapeDtypeStruct((rows // 4, cols), jnp.bfloat16)] * 4,
        compiler_params=pltpu.CompilerParams(vmem_limit_bytes=16 * MIB),
        cost_estimate=BRIEF,
        name="reduced",
    )(place, *slabs, after)


def cut_kernel(core_ref, total_ref, _, keep_ref, send_ref):
    rows = keep_ref.shape[0]
    keep_ref[...] = total_ref[pl.ds(pl.multiple_of(core_ref[0] * rows, rows), rows)]
    send_ref[...] = total_ref[pl.ds(pl.multiple_of((1 - core_ref[0]) * rows, rows), rows)]


def cut(core, total, after):
    rows, cols = total.shape
    whole = pl.BlockSpec(memory_space=pltpu.VMEM)
    return pl.pallas_call(
        cut_kernel,
        in_specs=[pl.BlockSpec(memory_space=pltpu.SMEM), whole, pl.BlockSpec(memory_space=pl.ANY)],
        out_specs=[whole] * 2,
        out_shape=[jax.ShapeDtypeStruct((rows // 2, cols), jnp.float32)] * 2,
        compiler_params=pltpu.CompilerParams(vmem_limit_bytes=12 * MIB),
        cost_estimate=BRIEF,
        name="cut",
    )(core, total, after)


def total_kernel(*refs):
    *in_refs, _, out_ref = refs
    rows = in_refs[0].shape[0]
    half = len(in_refs) // 2
    for n, group in enumerate((in_refs[:half], in_refs[half:])):
        total = 0.0
        for in_ref in group:
            total += in_ref[...].astype(jnp.float32)
        out_ref[n * rows : (n + 1) * rows] = total.astype(out_ref.dtype)


def totals(first, second, after):
    whole = pl.BlockSpec(memory_space=pltpu.VMEM)
    rows, cols = first[0].shape
    return pl.pallas_call(
        total_kernel,
        in_specs=[whole] * 2 * len(first) + [pl.BlockSpec(memory_space=pl.ANY)],
        out_specs=whole,
        out_shape=jax.ShapeDtypeStruct((2 * rows, cols), jnp.bfloat16),
        compiler_params=pltpu.CompilerParams(vmem_limit_bytes=16 * MIB),
        cost_estimate=BRIEF,
        name="totals",
    )(*first, *second, after)


def pair_kernel(mine_ref, other_ref, first_ref, second_ref):
    total = mine_ref[...].astype(jnp.float32) + other_ref[...].astype(jnp.float32)
    rows = first_ref.shape[0]
    first_ref[...] = total[:rows].astype(first_ref.dtype)
    second_ref[...] = total[rows:].astype(second_ref.dtype)


def pair_up(mine, other):
    whole = pl.BlockSpec(memory_space=pltpu.VMEM)
    rows, cols = mine.shape
    return pl.pallas_call(
        pair_kernel,
        in_specs=[whole, whole],
        out_specs=[whole, whole],
        out_shape=[jax.ShapeDtypeStruct((rows // 2, cols), mine.dtype)] * 2,
        compiler_params=pltpu.CompilerParams(vmem_limit_bytes=16 * MIB),
        cost_estimate=BRIEF,
        name="pair_up",
    )(mine, other)


def stack_kernel(*refs):
    *in_refs, _, first_ref, second_ref = refs
    rows = in_refs[0].shape[0]
    half = len(in_refs) // 2
    for out_ref, group in ((first_ref, in_refs[:half]), (second_ref, in_refs[half:])):
        for n, in_ref in enumerate(group):
            out_ref[n * rows : (n + 1) * rows] = in_ref[...]


def stack(first, second, after):
    whole = pl.BlockSpec(memory_space=pltpu.VMEM)
    rows, cols = first[0].shape
    return pl.pallas_call(
        stack_kernel,
        in_specs=[whole] * 2 * len(first) + [pl.BlockSpec(memory_space=pl.ANY)],
        out_specs=[whole, whole],
        out_shape=[jax.ShapeDtypeStruct((len(first) * rows, cols), first[0].dtype)] * 2,
        compiler_params=pltpu.CompilerParams(vmem_limit_bytes=16 * MIB),
        cost_estimate=BRIEF,
        name="stack",
    )(*first, *second, after)


def widen_kernel(place_ref, *refs):
    *slab_refs, _, _, uk_ref, uv_ref, wide_ref, sems = refs
    rows = slab_refs[0].shape[0] // len(HOPS)
    copies = []
    for n, slab_ref in enumerate(slab_refs):
        chunk, hop = n // len(HOPS), HOPS[n % len(HOPS)]
        outer, inner = place_ref[1 + chunk], place_ref[2 - chunk]
        for m, inner_hop in enumerate(HOPS):
            source = (inner - inner_hop + 4) % 4
            piece = slab_ref[m * rows : (m + 1) * rows].astype(jnp.float32)
            wide_ref[n, source % 2, source // 2] = piece
        head = 2 * (4 * chunk + (outer - hop + 4) % 4)
        for kind, out_ref in enumerate((uk_ref, uv_ref)):
            copy = pltpu.make_async_copy(wide_ref.at[n, kind], out_ref.at[pl.ds(head, 2)], sems.at[n, kind])
            copy.start()
            copies.append(copy)
    for copy in copies:
        copy.wait()


def widen(place, slabs, heads, height, after):
    cols = slabs[0].shape[1]
    whole = pl.BlockSpec(memory_space=pltpu.VMEM)
    somewhere = pl.BlockSpec(memory_space=pl.ANY)
    out = jax.ShapeDtypeStruct((heads, height, cols), jnp.float32)
    return pl.pallas_call(
        widen_kernel,
        in_specs=[pl.BlockSpec(memory_space=pltpu.SMEM)]
        + [whole] * len(slabs)
        + [somewhere] * len(after),
        out_specs=[somewhere] * 2,
        out_shape=[out, out],
        scratch_shapes=[
            pltpu.VMEM((len(slabs), 2, 2, height, cols), jnp.float32),
            pltpu.SemaphoreType.DMA((len(slabs), 2)),
        ],
        compiler_params=pltpu.CompilerParams(vmem_limit_bytes=20 * MIB),
        cost_estimate=pl.CostEstimate(flops=2**21, bytes_accessed=12 * MIB, transcendentals=0),
        name="widen",
    )(place, *slabs, *after)


def moved(block, along, back, far):
    route = []
    for x in range(4):
        for z in range(4):
            for y in range(2):
                to = ((x + along) % 4) * 8 + ((z + back) % 4) * 2 + (y + far) % 2
                route.append((x * 8 + z * 2 + y, to))
    return lax.ppermute(block, "ctx", route)


def along_x(blocks):
    return [moved(block, hop, 0, 0) for block, hop in zip(blocks, HOPS[1:])]


def along_z(blocks):
    return [moved(block, 0, hop, 0) for block, hop in zip(blocks, HOPS[1:])]


def swap_core(block):
    return lax.ppermute(block, "head", [(0, 1), (1, 0), (2, 3), (3, 2)])


def swap_far(block):
    return lax.ppermute(block, "head", [(0, 2), (2, 0), (1, 3), (3, 1)])


def body(latent, query, d_out, w_uk, w_uv, block_mask, segments):
    toks, lat = latent.shape
    heads, nope, rank = w_uk.shape
    width = query.shape[1] // heads
    inv_root = 1.0 / math.sqrt(width)
    position = lax.axis_index("ctx")
    seg_rows = segments.reshape(-1, toks)
    latent_t = latent.T
    blocks = [shifted(latent_t, "ctx", distance) for distance in (2, 1)] + [latent_t]
    qfull, dlo, dout_t, nope_t = prepare(query, d_out, w_uk, w_uv)

    core = (lax.axis_index("head") % 2).astype(jnp.int32).reshape(1)
    carried = []
    slabs = []
    count = heads // CHUNKS
    place = jnp.stack([position, position // 8, position // 2 % 4]).astype(jnp.int32)
    for chunk in range(CHUNKS):
        outputs = score(
            1 + chunk,
            place,
            block_mask,
            seg_rows,
            blocks,
            qfull,
            dlo,
            dout_t,
            nope_t,
            inv_root,
            chunk * count,
            count,
            carried,
        )
        carried = outputs[:4]
        slabs.append(outputs[4:])
    probs, dscore, lout, dfull = carried
    first, second = slabs
    first = reduced(2, place, [first[0]] + along_x(first[1:]), probs)
    total = key_gradient(qfull, dlo, probs, dscore, first[0])
    second = reduced(1, place, [second[0]] + along_z(second[1:]), total)
    keep, send = cut(core, total, second[0])
    own, *parts = split(keep, swap_core(send), toks)
    mine = totals([first[0]] + along_z(first[1:]), [second[0]] + along_x(second[1:]), own)
    low = merge(own, [shifted(parts[part], "ctx", part - SPAN) for part in range(SPAN)])
    first, second = pair_up(mine, moved(mine, 0, 0, 1))
    half = finish(low, swap_far(low))
    first, second = stack([first] + along_z([first] * 3), [second] + along_x([second] * 3), half)
    attended, d_query = project(lout, dfull, w_uk, w_uv, first)
    d_latent_t = assemble(core, half, swap_core(half))
    slabs = [first] + along_x([first] * 3) + [second] + along_z([second] * 3)
    d_w_uk, d_w_uv = widen(place, slabs, heads, nope, (attended, d_latent_t))
    return attended, d_query, d_latent_t.T, d_w_uk, d_w_uv


def solution(mesh):
    in_specs = (
        P("ctx", None),
        P("ctx", "head"),
        P("ctx", "head"),
        P("head", None, None),
        P("head", None, None),
        P(),
        P(),
    )
    out_specs = (
        P("ctx", "head"),
        P("ctx", "head"),
        P("ctx", None),
        P("head", None, None),
        P("head", None, None),
    )
    return jax.shard_map(body, mesh=mesh, in_specs=in_specs, out_specs=out_specs, check_vma=False)
```

```python
import functools
import math

import jax
import jax.numpy as jnp
from jax import lax
from jax.experimental import pallas as pl
from jax.experimental.pallas import tpu as pltpu
from jax.sharding import PartitionSpec as P

SPAN = 2
CHUNKS = 2
HOPS = (0, 1, -1, 2)
GROUP = 4
LOG2E = 1.4426950408889634
MIB = 2**20
LARGE = 56 * MIB
BRIEF = pl.CostEstimate(flops=2**20, bytes_accessed=2**20, transcendentals=0)


def shifted(block, axis, distance):
    devices = range(lax.axis_size(axis))
    route = [(i - distance, i) for i in devices if i - distance in devices]
    return lax.ppermute(block, axis, route)

TOKEN = jax.ShapeDtypeStruct((8, 128), jnp.float32)
WHOLE = pl.BlockSpec(memory_space=pltpu.VMEM)
TOKEN_BLOCK = pl.BlockSpec((8, 128), lambda *_: (0, 0))


def with_token(kernel, scratch=0):
    def wrapped(*refs):
        end = len(refs) - scratch
        refs[end - 1][...] = jnp.zeros(TOKEN.shape, TOKEN.dtype)
        kernel(*refs[: end - 1], *refs[end:])

    return wrapped


def dot(a, b):
    return lax.dot_general(a, b, (((1,), (0,)), ((), ())), preferred_element_type=jnp.float32)


def dot_nt(a, b):
    return lax.dot_general(a, b, (((1,), (1,)), ((), ())), preferred_element_type=jnp.float32)


def prepare_kernel(query_ref, dout_ref, wuk_ref, wuv_ref, qfull_ref, dlo_ref, dout_t_ref, nope_t_ref):
    nope = wuk_ref.shape[1]
    value = wuv_ref.shape[1]
    width = query_ref.shape[1] // wuk_ref.shape[0]
    rank = wuk_ref.shape[2]
    toks = query_ref.shape[0]
    query_t = query_ref[...].T
    dout_t = dout_ref[...].T
    for n in range(wuk_ref.shape[0]):
        q_nope = query_t[n * width : n * width + nope]
        grads = dout_t[n * value : (n + 1) * value]
        span = slice(n * toks, (n + 1) * toks)
        nope_t_ref[:, span] = q_nope
        dout_t_ref[:, span] = grads
        qfull_ref[:rank, span] = dot(wuk_ref[n].T, q_nope).astype(jnp.bfloat16)
        qfull_ref[rank:, span] = query_t[n * width + nope : (n + 1) * width]
        dlo_ref[:, span] = dot(wuv_ref[n].T, grads).astype(jnp.bfloat16)


def prepare(query, d_out, w_uk, w_uv):
    toks = query.shape[0]
    heads, nope, rank = w_uk.shape
    value = w_uv.shape[1]
    width = query.shape[1] // heads
    lat = rank + width - nope
    shape = lambda rows: jax.ShapeDtypeStruct((rows, heads * toks), jnp.bfloat16)
    block = lambda rows: pl.BlockSpec((rows, GROUP * toks), lambda s: (0, s))
    return pl.pallas_call(
        prepare_kernel,
        grid=(heads // GROUP,),
        in_specs=[
            pl.BlockSpec((toks, GROUP * width), lambda s: (0, s)),
            pl.BlockSpec((toks, GROUP * value), lambda s: (0, s)),
            pl.BlockSpec((GROUP, nope, rank), lambda s: (s, 0, 0)),
            pl.BlockSpec((GROUP, value, rank), lambda s: (s, 0, 0)),
        ],
        out_specs=[block(lat), block(rank), block(value), block(nope)],
        out_shape=[shape(lat), shape(rank), shape(value), shape(nope)],
        compiler_params=pltpu.CompilerParams(vmem_limit_bytes=LARGE),
        cost_estimate=pl.CostEstimate(
            flops=4 * heads * toks * nope * rank, bytes_accessed=16 * 2**20, transcendentals=0
        ),
        name="prepare",
    )(query, d_out, w_uk, w_uv)


def score_kernel(
    inv_root,
    which,
    place_ref,
    mask_ref,
    segments_ref,
    block_refs,
    qfull_ref,
    dlo_ref,
    dout_t_ref,
    nope_t_ref,
    *rest,
):
    probs_ref, dscore_ref, lout_ref, dfull_ref, *slab_refs, grad_ref, keys_ref, keys_t_ref, bias_ref = rest[-12:]
    rank = dlo_ref.shape[0]
    toks = block_refs[0].shape[1]
    group = range(qfull_ref.shape[1] // toks)
    step = pl.program_id(0)

    @pl.when(step == 0)
    def _():
        for n, block_ref in enumerate(block_refs):
            keys_t_ref[:, n * toks : (n + 1) * toks] = block_ref[...]
            keys_ref[n * toks : (n + 1) * toks] = block_ref[...].T
        position = place_ref[0]
        seg_query = segments_ref[pl.ds(position, 1)].astype(jnp.float32)
        for n in range(len(block_refs)):
            distance = len(block_refs) - 1 - n
            block = jnp.maximum(position - distance, 0)
            seg_row = segments_ref[pl.ds(block, 1)].astype(jnp.float32)
            seg_key = jnp.broadcast_to(seg_row, (toks, toks)).T
            granted = jnp.broadcast_to(mask_ref[position, block], (toks, toks)) == 1
            allowed = (seg_key == seg_query) | granted
            if distance == 0:
                key, query = (lax.broadcasted_iota(jnp.int32, (toks, toks), axis) for axis in (0, 1))
                allowed &= key <= query
            else:
                allowed &= jnp.broadcast_to(position, (toks, toks)) >= distance
            bias_ref[n * toks : (n + 1) * toks] = jnp.where(allowed, 0.0, -jnp.inf)

    def slab(n):
        return (step * (len(group) // 2) + n // 2 + 4 - place_ref[which]) % 4

    part = lambda ref, n: ref[:, n * toks : (n + 1) * toks]
    scores = dot(keys_ref[...], qfull_ref[...])
    probs = []
    for n in group:
        scaled = scores[:, n * toks : (n + 1) * toks] * (inv_root * LOG2E) + bias_ref[...]
        weights = jnp.exp2(scaled - jnp.max(scaled, axis=0, keepdims=True))
        probs.append(weights * (1.0 / jnp.sum(weights, axis=0, keepdims=True)))
        probs_ref[:, n * toks : (n + 1) * toks] = probs[n].astype(jnp.bfloat16)
    d_probs = dot(keys_ref[:, :rank], dlo_ref[...])
    lout_ref[...] = dot(keys_t_ref[:rank], probs_ref[...]).astype(jnp.bfloat16)
    for n in group:
        d_prob = d_probs[:, n * toks : (n + 1) * toks]
        delta = jnp.sum(probs[n] * d_prob, axis=0, keepdims=True)
        d_score = probs[n] * (d_prob - delta) * inv_root
        dscore_ref[:, n * toks : (n + 1) * toks] = d_score.astype(jnp.bfloat16)
    for n in group:
        grad_ref[slab(n), n % 2, 1] = dot_nt(part(dout_t_ref, n), part(lout_ref, n)).astype(jnp.bfloat16)
    dfull_ref[...] = dot(keys_t_ref[...], dscore_ref[...]).astype(jnp.bfloat16)
    for n in group:
        d_absorbed = dfull_ref[:rank, n * toks : (n + 1) * toks]
        grad_ref[slab(n), n % 2, 0] = dot_nt(part(nope_t_ref, n), d_absorbed).astype(jnp.bfloat16)

    @pl.when(step == pl.num_programs(0) - 1)
    def _():
        for hop, slab_ref in zip(HOPS, slab_refs):
            slab_ref[...] = grad_ref[hop % 4].reshape(slab_ref.shape)


def score(which, place, block_mask, segments, blocks, qfull, dlo, dout_t, nope_t, inv_root, start, count, carried):
    lat, toks = blocks[0].shape
    heads = qfull.shape[1] // toks
    span = len(blocks) * toks
    rank = dlo.shape[0]
    value, nope = dout_t.shape[0], nope_t.shape[0]
    base = start // GROUP
    whole = lambda rows, cols: pl.BlockSpec((rows, cols), lambda s: (0, 0))
    heads_of = lambda rows: pl.BlockSpec((rows, GROUP * toks), lambda s: (0, s + base))
    out = lambda rows: jax.ShapeDtypeStruct((rows, heads * toks), jnp.bfloat16)
    return pl.pallas_call(
        with_token(functools.partial(score_kernel, inv_root, which), 4),
        grid=(count // GROUP,),
        in_specs=[
            pl.BlockSpec(memory_space=pltpu.SMEM),
            pl.BlockSpec(memory_space=pltpu.SMEM),
            whole(*segments.shape),
            [whole(lat, toks)] * len(blocks),
            heads_of(lat),
            heads_of(rank),
            heads_of(value),
            heads_of(nope),
        ]
        + [pl.BlockSpec(memory_space=pl.ANY)] * len(carried),
        out_specs=[
            heads_of(span),
            heads_of(span),
            heads_of(rank),
            heads_of(lat),
        ]
        + [whole(4 * nope, rank)] * len(HOPS)
        + [TOKEN_BLOCK],
        out_shape=[
            out(span),
            out(span),
            out(rank),
            out(lat),
        ]
        + [jax.ShapeDtypeStruct((4 * nope, rank), jnp.bfloat16)] * len(HOPS)
        + [TOKEN],
        input_output_aliases={7 + len(blocks) + n: n for n in range(len(carried))},
        scratch_shapes=[
            pltpu.VMEM((4, 2, 2, nope, rank), jnp.bfloat16),
            pltpu.VMEM((span, lat), jnp.bfloat16),
            pltpu.VMEM((lat, span), jnp.bfloat16),
            pltpu.VMEM((span, toks), jnp.float32),
        ],
        compiler_params=pltpu.CompilerParams(vmem_limit_bytes=56 * MIB),
        cost_estimate=pl.CostEstimate(
            flops=8 * count * toks * span * (rank + lat),
            bytes_accessed=3 * count * 2**20,
            transcendentals=count * toks * span,
        ),
        name="score",
    )(place, block_mask, segments, blocks, qfull, dlo, dout_t, nope_t, *carried)


def key_kernel(qfull_ref, dlo_ref, probs_ref, dscore_ref, _, total_ref):
    rank = dlo_ref.shape[0]

    @pl.when(pl.program_id(0) == 0)
    def _():
        total_ref[...] = jnp.zeros_like(total_ref)

    total_ref[:rank] += dot_nt(qfull_ref[:rank], dscore_ref[...]) + dot_nt(dlo_ref[...], probs_ref[...])
    total_ref[rank:] += dot_nt(qfull_ref[rank:], dscore_ref[...])


def key_gradient(qfull, dlo, probs, dscore, toks, after):
    lat, rank, span = qfull.shape[0], dlo.shape[0], probs.shape[0]
    heads = qfull.shape[1] // toks
    heads_of = lambda rows: pl.BlockSpec((rows, GROUP * toks), lambda s: (0, s))
    return pl.pallas_call(
        with_token(key_kernel),
        grid=(heads // GROUP,),
        in_specs=[heads_of(lat), heads_of(rank), heads_of(span), heads_of(span)]
        + [pl.BlockSpec(memory_space=pl.ANY)],
        out_specs=[pl.BlockSpec((lat, span), lambda s: (0, 0)), TOKEN_BLOCK],
        out_shape=[jax.ShapeDtypeStruct((lat, span), jnp.float32), TOKEN],
        compiler_params=pltpu.CompilerParams(vmem_limit_bytes=LARGE),
        cost_estimate=pl.CostEstimate(
            flops=4 * heads * toks * span * (rank + lat), bytes_accessed=24 * MIB, transcendentals=0
        ),
        name="key_gradient",
    )(qfull, dlo, probs, dscore, after)


def split_kernel(keep_ref, got_ref, own_ref, *part_refs):
    toks = own_ref.shape[1]
    for part, part_ref in enumerate(part_refs + (own_ref,)):
        span = slice(part * toks, (part + 1) * toks)
        part_ref[...] = (keep_ref[:, span] + got_ref[:, span]).astype(part_ref.dtype)


def split(keep, got, toks):
    rows, span = keep.shape
    out = lambda dtype: jax.ShapeDtypeStruct((rows, toks), dtype)
    return pl.pallas_call(
        with_token(split_kernel),
        out_shape=[out(jnp.float32)] + [out(jnp.bfloat16)] * SPAN + [TOKEN],
        compiler_params=pltpu.CompilerParams(vmem_limit_bytes=12 * MIB),
        cost_estimate=BRIEF,
        name="split",
    )(keep, got)


def merge_kernel(own_ref, *rest):
    *part_refs, out_ref = rest
    total = own_ref[...]
    for part_ref in part_refs:
        total += part_ref[...].astype(jnp.float32)
    out_ref[...] = total.astype(out_ref.dtype)


def merge(own, parts):
    return pl.pallas_call(
        merge_kernel,
        out_shape=jax.ShapeDtypeStruct(own.shape, jnp.bfloat16),
        compiler_params=pltpu.CompilerParams(vmem_limit_bytes=12 * MIB),
        cost_estimate=BRIEF,
        name="merge",
    )(own, *parts)


def finish_kernel(own_ref, far_ref, out_ref):
    out_ref[...] = own_ref[...].astype(jnp.float32) + far_ref[...].astype(jnp.float32)


def finish(own, far):
    return pl.pallas_call(
        with_token(finish_kernel),
        out_shape=[jax.ShapeDtypeStruct(own.shape, jnp.float32), TOKEN],
        compiler_params=pltpu.CompilerParams(vmem_limit_bytes=12 * MIB),
        cost_estimate=BRIEF,
        name="finish",
    )(own, far)


def assemble_kernel(core_ref, mine_ref, other_ref, out_ref):
    rows = mine_ref.shape[0]
    core = core_ref[0]
    out_ref[pl.ds(pl.multiple_of(core * rows, rows), rows)] = mine_ref[...]
    out_ref[pl.ds(pl.multiple_of((1 - core) * rows, rows), rows)] = other_ref[...]


def assemble(core, mine, other):
    rows, toks = mine.shape
    whole = pl.BlockSpec(memory_space=pltpu.VMEM)
    return pl.pallas_call(
        with_token(assemble_kernel),
        in_specs=[pl.BlockSpec(memory_space=pltpu.SMEM), whole, whole],
        out_specs=[whole] * 2,
        out_shape=[jax.ShapeDtypeStruct((2 * rows, toks), jnp.float32), TOKEN],
        compiler_params=pltpu.CompilerParams(vmem_limit_bytes=12 * MIB),
        cost_estimate=BRIEF,
        name="assemble",
    )(core, mine, other)


def project_kernel(lout_ref, dfull_ref, wuk_ref, wuv_ref, _, att_ref, dq_ref):
    group = range(wuk_ref.shape[0])
    rank = lout_ref.shape[0]
    toks = att_ref.shape[0]
    value = wuv_ref.shape[1]
    width = dq_ref.shape[1] // len(group)
    for n in group:
        attended = dot(wuv_ref[n], lout_ref[:, n * toks : (n + 1) * toks]).astype(jnp.bfloat16)
        att_ref[:, n * value : (n + 1) * value] = attended.T
        d_full = dfull_ref[:, n * toks : (n + 1) * toks]
        d_nope = dot(wuk_ref[n], d_full[:rank]).astype(jnp.bfloat16)
        dq_ref[:, n * width : (n + 1) * width] = jnp.concatenate([d_nope, d_full[rank:]], axis=0).T


def project(lout, dfull, w_uk, w_uv, after):
    heads, nope, rank = w_uk.shape
    lat, toks = dfull.shape[0], dfull.shape[1] // heads
    value = w_uv.shape[1]
    width = nope + lat - rank
    heads_of = lambda rows, cols: pl.BlockSpec((GROUP, rows, cols), lambda s: (s, 0, 0))
    wide = lambda rows: pl.BlockSpec((rows, GROUP * toks), lambda s: (0, s))
    out = lambda cols: jax.ShapeDtypeStruct((toks, heads * cols), jnp.bfloat16)
    return pl.pallas_call(
        with_token(project_kernel),
        grid=(heads // GROUP,),
        in_specs=[wide(rank), wide(lat), heads_of(nope, rank), heads_of(value, rank)]
        + [pl.BlockSpec(memory_space=pl.ANY)],
        out_specs=[
            pl.BlockSpec((toks, GROUP * value), lambda s: (0, s)),
            pl.BlockSpec((toks, GROUP * width), lambda s: (0, s)),
            TOKEN_BLOCK,
        ],
        out_shape=[out(value), out(width), TOKEN],
        compiler_params=pltpu.CompilerParams(vmem_limit_bytes=16 * MIB),
        cost_estimate=BRIEF,
        name="project",
    )(lout, dfull, w_uk, w_uv, after)


def reduce_kernel(which, place_ref, *refs):
    *slab_refs, _, own_ref, up_ref, down_ref, far_ref = refs
    rows = own_ref.shape[0]
    for hop, out_ref in zip(HOPS, (own_ref, up_ref, down_ref, far_ref)):
        span = pl.ds(pl.multiple_of(((place_ref[which] + hop + 4) % 4) * rows, rows), rows)
        total = 0.0
        for slab_ref in slab_refs:
            total += slab_ref[span].astype(jnp.float32)
        out_ref[...] = total.astype(out_ref.dtype)


def reduced(which, place, slabs, after):
    whole = pl.BlockSpec(memory_space=pltpu.VMEM)
    rows, cols = slabs[0].shape
    return pl.pallas_call(
        with_token(functools.partial(reduce_kernel, which)),
        in_specs=[pl.BlockSpec(memory_space=pltpu.SMEM)]
        + [whole] * len(slabs)
        + [pl.BlockSpec(memory_space=pl.ANY)],
        out_specs=[whole] * 5,
        out_shape=[jax.ShapeDtypeStruct((rows // 4, cols), jnp.bfloat16)] * 4 + [TOKEN],
        compiler_params=pltpu.CompilerParams(vmem_limit_bytes=16 * MIB),
        cost_estimate=BRIEF,
        name="reduced",
    )(place, *slabs, after)


def cut_kernel(core_ref, total_ref, _, keep_ref, send_ref):
    rows = keep_ref.shape[0]
    keep_ref[...] = total_ref[pl.ds(pl.multiple_of(core_ref[0] * rows, rows), rows)]
    send_ref[...] = total_ref[pl.ds(pl.multiple_of((1 - core_ref[0]) * rows, rows), rows)]


def cut(core, total, after):
    rows, cols = total.shape
    whole = pl.BlockSpec(memory_space=pltpu.VMEM)
    return pl.pallas_call(
        cut_kernel,
        in_specs=[pl.BlockSpec(memory_space=pltpu.SMEM), whole, pl.BlockSpec(memory_space=pl.ANY)],
        out_specs=[whole] * 2,
        out_shape=[jax.ShapeDtypeStruct((rows // 2, cols), jnp.float32)] * 2,
        compiler_params=pltpu.CompilerParams(vmem_limit_bytes=12 * MIB),
        cost_estimate=BRIEF,
        name="cut",
    )(core, total, after)


def total_kernel(*refs):
    *in_refs, _, out_ref = refs
    rows = in_refs[0].shape[0]
    half = len(in_refs) // 2
    for n, group in enumerate((in_refs[:half], in_refs[half:])):
        total = 0.0
        for in_ref in group:
            total += in_ref[...].astype(jnp.float32)
        out_ref[n * rows : (n + 1) * rows] = total.astype(out_ref.dtype)


def totals(first, second, after):
    whole = pl.BlockSpec(memory_space=pltpu.VMEM)
    rows, cols = first[0].shape
    return pl.pallas_call(
        total_kernel,
        in_specs=[whole] * 2 * len(first) + [pl.BlockSpec(memory_space=pl.ANY)],
        out_specs=whole,
        out_shape=jax.ShapeDtypeStruct((2 * rows, cols), jnp.bfloat16),
        compiler_params=pltpu.CompilerParams(vmem_limit_bytes=16 * MIB),
        cost_estimate=BRIEF,
        name="totals",
    )(*first, *second, after)


def pair_kernel(mine_ref, other_ref, first_ref, second_ref):
    total = mine_ref[...].astype(jnp.float32) + other_ref[...].astype(jnp.float32)
    rows = first_ref.shape[0]
    first_ref[...] = total[:rows].astype(first_ref.dtype)
    second_ref[...] = total[rows:].astype(second_ref.dtype)


def pair_up(mine, other):
    whole = pl.BlockSpec(memory_space=pltpu.VMEM)
    rows, cols = mine.shape
    return pl.pallas_call(
        pair_kernel,
        in_specs=[whole, whole],
        out_specs=[whole, whole],
        out_shape=[jax.ShapeDtypeStruct((rows // 2, cols), mine.dtype)] * 2,
        compiler_params=pltpu.CompilerParams(vmem_limit_bytes=16 * MIB),
        cost_estimate=BRIEF,
        name="pair_up",
    )(mine, other)


def stack_kernel(*refs):
    *in_refs, _, first_ref, second_ref = refs
    rows = in_refs[0].shape[0]
    half = len(in_refs) // 2
    for out_ref, group in ((first_ref, in_refs[:half]), (second_ref, in_refs[half:])):
        for n, in_ref in enumerate(group):
            out_ref[n * rows : (n + 1) * rows] = in_ref[...]


def stack(first, second, after):
    whole = pl.BlockSpec(memory_space=pltpu.VMEM)
    rows, cols = first[0].shape
    return pl.pallas_call(
        with_token(stack_kernel),
        in_specs=[whole] * 2 * len(first) + [pl.BlockSpec(memory_space=pl.ANY)],
        out_specs=[whole] * 3,
        out_shape=[jax.ShapeDtypeStruct((len(first) * rows, cols), first[0].dtype)] * 2 + [TOKEN],
        compiler_params=pltpu.CompilerParams(vmem_limit_bytes=16 * MIB),
        cost_estimate=BRIEF,
        name="stack",
    )(*first, *second, after)


def widen_kernel(chunk, place_ref, *refs):
    slab_refs = refs[: len(HOPS)]
    uk_ref, uv_ref, wide_ref, sems = refs[-4:]
    rows = slab_refs[0].shape[0] // len(HOPS)
    outer, inner = place_ref[1 + chunk], place_ref[2 - chunk]
    copies = []
    for n, slab_ref in enumerate(slab_refs):
        for m, hop in enumerate(HOPS):
            source = (inner - hop + 4) % 4
            wide_ref[n, source % 2, source // 2] = slab_ref[m * rows : (m + 1) * rows].astype(jnp.float32)
        head = 2 * (4 * chunk + (outer - HOPS[n] + 4) % 4)
        for kind, out_ref in enumerate((uk_ref, uv_ref)):
            copy = pltpu.make_async_copy(wide_ref.at[n, kind], out_ref.at[pl.ds(head, 2)], sems.at[n, kind])
            copy.start()
            copies.append(copy)
    for copy in copies:
        copy.wait()


def widen(chunk, place, slabs, heads, height, after, carried):
    cols = slabs[0].shape[1]
    somewhere = pl.BlockSpec(memory_space=pl.ANY)
    out = jax.ShapeDtypeStruct((heads, height, cols), jnp.float32)
    return pl.pallas_call(
        functools.partial(widen_kernel, chunk),
        in_specs=[pl.BlockSpec(memory_space=pltpu.SMEM)]
        + [WHOLE] * len(slabs)
        + [somewhere] * (1 + len(carried)),
        out_specs=[somewhere] * 2,
        out_shape=[out, out],
        input_output_aliases={2 + len(slabs) + n: n for n in range(len(carried))},
        scratch_shapes=[
            pltpu.VMEM((len(slabs), 2, 2, height, cols), jnp.float32),
            pltpu.SemaphoreType.DMA((len(slabs), 2)),
        ],
        compiler_params=pltpu.CompilerParams(vmem_limit_bytes=12 * MIB),
        cost_estimate=BRIEF,
        name="widen",
    )(place, *slabs, after, *carried)


def moved(block, along, back, far):
    route = []
    for x in range(4):
        for z in range(4):
            for y in range(2):
                to = ((x + along) % 4) * 8 + ((z + back) % 4) * 2 + (y + far) % 2
                route.append((x * 8 + z * 2 + y, to))
    return lax.ppermute(block, "ctx", route)


def along_x(blocks):
    return [moved(block, hop, 0, 0) for block, hop in zip(blocks, HOPS[1:])]


def along_z(blocks):
    return [moved(block, 0, hop, 0) for block, hop in zip(blocks, HOPS[1:])]


def swap_core(block):
    return lax.ppermute(block, "head", [(0, 1), (1, 0), (2, 3), (3, 2)])


def swap_far(block):
    return lax.ppermute(block, "head", [(0, 2), (2, 0), (1, 3), (3, 1)])


def body(latent, query, d_out, w_uk, w_uv, block_mask, segments):
    toks, lat = latent.shape
    heads, nope, rank = w_uk.shape
    width = query.shape[1] // heads
    inv_root = 1.0 / math.sqrt(width)
    position = lax.axis_index("ctx")
    seg_rows = segments.reshape(-1, toks)
    latent_t = latent.T
    blocks = [shifted(latent_t, "ctx", distance) for distance in (2, 1)] + [latent_t]
    qfull, dlo, dout_t, nope_t = prepare(query, d_out, w_uk, w_uv)

    core = (lax.axis_index("head") % 2).astype(jnp.int32).reshape(1)
    carried = []
    slabs = []
    count = heads // CHUNKS
    place = jnp.stack([position, position // 8, position // 2 % 4]).astype(jnp.int32)
    for chunk in range(CHUNKS):
        outputs = score(
            1 + chunk,
            place,
            block_mask,
            seg_rows,
            blocks,
            qfull,
            dlo,
            dout_t,
            nope_t,
            inv_root,
            chunk * count,
            count,
            carried,
        )
        carried = outputs[:4]
        slabs.append(outputs[4:8])
        token = outputs[8]
    probs, dscore, lout, dfull = carried
    first, second = slabs
    *first, token = reduced(2, place, [first[0]] + along_x(first[1:]), token)
    total, token = key_gradient(qfull, dlo, probs, dscore, toks, token)
    *second, token = reduced(1, place, [second[0]] + along_z(second[1:]), token)
    keep, send = cut(core, total, token)
    own, *parts, token = split(keep, swap_core(send), toks)
    mine = totals([first[0]] + along_z(first[1:]), [second[0]] + along_x(second[1:]), token)
    low = merge(own, [shifted(parts[part], "ctx", part - SPAN) for part in range(SPAN)])
    first, second = pair_up(mine, moved(mine, 0, 0, 1))
    half, token = finish(low, swap_far(low))
    d_latent_t, token = assemble(core, half, swap_core(half))
    first, second, token = stack([first] + along_z([first] * 3), [second] + along_x([second] * 3), token)
    attended, d_query, token = project(lout, dfull, w_uk, w_uv, token)
    grads = widen(0, place, [first] + along_x([first] * 3), heads, nope, token, [])
    d_w_uk, d_w_uv = widen(1, place, [second] + along_z([second] * 3), heads, nope, token, grads)
    return attended, d_query, d_latent_t.T, d_w_uk, d_w_uv


def solution(mesh):
    in_specs = (
        P("ctx", None),
        P("ctx", "head"),
        P("ctx", "head"),
        P("head", None, None),
        P("head", None, None),
        P(),
        P(),
    )
    out_specs = (
        P("ctx", "head"),
        P("ctx", "head"),
        P("ctx", None),
        P("head", None, None),
        P("head", None, None),
    )
    return jax.shard_map(body, mesh=mesh, in_specs=in_specs, out_specs=out_specs, check_vma=False)
```

```python
import functools
import math

import jax
import jax.numpy as jnp
from jax import lax
from jax.experimental import pallas as pl
from jax.experimental.pallas import tpu as pltpu
from jax.sharding import PartitionSpec as P

SPAN = 2
CHUNKS = 2
HOPS = (0, 1, -1, 2)
GROUP = 4
LOG2E = 1.4426950408889634
MIB = 2**20
LARGE = 56 * MIB
BRIEF = pl.CostEstimate(flops=2**20, bytes_accessed=2**20, transcendentals=0)


def shifted(block, axis, distance):
    devices = range(lax.axis_size(axis))
    route = [(i - distance, i) for i in devices if i - distance in devices]
    return lax.ppermute(block, axis, route)

TOKEN = jax.ShapeDtypeStruct((8, 128), jnp.float32)
WHOLE = pl.BlockSpec(memory_space=pltpu.VMEM)
TOKEN_BLOCK = pl.BlockSpec((8, 128), lambda *_: (0, 0))


def with_token(kernel, scratch=0):
    def wrapped(*refs):
        end = len(refs) - scratch
        refs[end - 1][...] = jnp.zeros(TOKEN.shape, TOKEN.dtype)
        kernel(*refs[: end - 1], *refs[end:])

    return wrapped


def dot(a, b):
    return lax.dot_general(a, b, (((1,), (0,)), ((), ())), preferred_element_type=jnp.float32)


def dot_nt(a, b):
    return lax.dot_general(a, b, (((1,), (1,)), ((), ())), preferred_element_type=jnp.float32)


def prepare_kernel(query_ref, dout_ref, wuk_ref, wuv_ref, qfull_ref, dlo_ref, dout_t_ref, nope_t_ref):
    nope = wuk_ref.shape[1]
    value = wuv_ref.shape[1]
    width = query_ref.shape[1] // wuk_ref.shape[0]
    rank = wuk_ref.shape[2]
    toks = query_ref.shape[0]
    query_t = query_ref[...].T
    dout_t = dout_ref[...].T
    for n in range(wuk_ref.shape[0]):
        q_nope = query_t[n * width : n * width + nope]
        grads = dout_t[n * value : (n + 1) * value]
        span = slice(n * toks, (n + 1) * toks)
        nope_t_ref[:, span] = q_nope
        dout_t_ref[:, span] = grads
        qfull_ref[:rank, span] = dot(wuk_ref[n].T, q_nope).astype(jnp.bfloat16)
        qfull_ref[rank:, span] = query_t[n * width + nope : (n + 1) * width]
        dlo_ref[:, span] = dot(wuv_ref[n].T, grads).astype(jnp.bfloat16)


def prepare(query, d_out, w_uk, w_uv):
    toks = query.shape[0]
    heads, nope, rank = w_uk.shape
    value = w_uv.shape[1]
    width = query.shape[1] // heads
    lat = rank + width - nope
    shape = lambda rows: jax.ShapeDtypeStruct((rows, heads * toks), jnp.bfloat16)
    block = lambda rows: pl.BlockSpec((rows, GROUP * toks), lambda s: (0, s))
    return pl.pallas_call(
        prepare_kernel,
        grid=(heads // GROUP,),
        in_specs=[
            pl.BlockSpec((toks, GROUP * width), lambda s: (0, s)),
            pl.BlockSpec((toks, GROUP * value), lambda s: (0, s)),
            pl.BlockSpec((GROUP, nope, rank), lambda s: (s, 0, 0)),
            pl.BlockSpec((GROUP, value, rank), lambda s: (s, 0, 0)),
        ],
        out_specs=[block(lat), block(rank), block(value), block(nope)],
        out_shape=[shape(lat), shape(rank), shape(value), shape(nope)],
        compiler_params=pltpu.CompilerParams(vmem_limit_bytes=LARGE),
        cost_estimate=pl.CostEstimate(
            flops=4 * heads * toks * nope * rank, bytes_accessed=16 * 2**20, transcendentals=0
        ),
        name="prepare",
    )(query, d_out, w_uk, w_uv)


def score_kernel(
    inv_root,
    which,
    place_ref,
    mask_ref,
    segments_ref,
    block_refs,
    qfull_ref,
    dlo_ref,
    dout_t_ref,
    nope_t_ref,
    *rest,
):
    probs_ref, dscore_ref, lout_ref, dfull_ref, *slab_refs, grad_ref, keys_ref, keys_t_ref, bias_ref = rest[-12:]
    rank = dlo_ref.shape[0]
    toks = block_refs[0].shape[1]
    group = range(qfull_ref.shape[1] // toks)
    step = pl.program_id(0)

    @pl.when(step == 0)
    def _():
        for n, block_ref in enumerate(block_refs):
            keys_t_ref[:, n * toks : (n + 1) * toks] = block_ref[...]
            keys_ref[n * toks : (n + 1) * toks] = block_ref[...].T
        position = place_ref[0]
        seg_query = segments_ref[pl.ds(position, 1)].astype(jnp.float32)
        for n in range(len(block_refs)):
            distance = len(block_refs) - 1 - n
            block = jnp.maximum(position - distance, 0)
            seg_row = segments_ref[pl.ds(block, 1)].astype(jnp.float32)
            seg_key = jnp.broadcast_to(seg_row, (toks, toks)).T
            granted = jnp.broadcast_to(mask_ref[position, block], (toks, toks)) == 1
            allowed = (seg_key == seg_query) | granted
            if distance == 0:
                key, query = (lax.broadcasted_iota(jnp.int32, (toks, toks), axis) for axis in (0, 1))
                allowed &= key <= query
            else:
                allowed &= jnp.broadcast_to(position, (toks, toks)) >= distance
            bias_ref[n * toks : (n + 1) * toks] = jnp.where(allowed, 0.0, -jnp.inf)

    def slab(n):
        return (step * (len(group) // 2) + n // 2 + 4 - place_ref[which]) % 4

    part = lambda ref, n: ref[:, n * toks : (n + 1) * toks]
    scores = dot(keys_ref[...], qfull_ref[...])
    probs = []
    for n in group:
        scaled = scores[:, n * toks : (n + 1) * toks] * (inv_root * LOG2E) + bias_ref[...]
        weights = jnp.exp2(scaled - jnp.max(scaled, axis=0, keepdims=True))
        probs.append(weights * (1.0 / jnp.sum(weights, axis=0, keepdims=True)))
        probs_ref[:, n * toks : (n + 1) * toks] = probs[n].astype(jnp.bfloat16)
    d_probs = dot(keys_ref[:, :rank], dlo_ref[...])
    lout_ref[...] = dot(keys_t_ref[:rank], probs_ref[...]).astype(jnp.bfloat16)
    for n in group:
        d_prob = d_probs[:, n * toks : (n + 1) * toks]
        delta = jnp.sum(probs[n] * d_prob, axis=0, keepdims=True)
        d_score = probs[n] * (d_prob - delta) * inv_root
        dscore_ref[:, n * toks : (n + 1) * toks] = d_score.astype(jnp.bfloat16)
    for n in group:
        grad_ref[slab(n), n % 2, 1] = dot_nt(part(dout_t_ref, n), part(lout_ref, n)).astype(jnp.bfloat16)
    dfull_ref[...] = dot(keys_t_ref[...], dscore_ref[...]).astype(jnp.bfloat16)
    for n in group:
        d_absorbed = dfull_ref[:rank, n * toks : (n + 1) * toks]
        grad_ref[slab(n), n % 2, 0] = dot_nt(part(nope_t_ref, n), d_absorbed).astype(jnp.bfloat16)

    @pl.when(step == pl.num_programs(0) - 1)
    def _():
        for hop, slab_ref in zip(HOPS, slab_refs):
            slab_ref[...] = grad_ref[hop % 4].reshape(slab_ref.shape)


def score(which, place, block_mask, segments, blocks, qfull, dlo, dout_t, nope_t, inv_root, start, count, carried):
    lat, toks = blocks[0].shape
    heads = qfull.shape[1] // toks
    span = len(blocks) * toks
    rank = dlo.shape[0]
    value, nope = dout_t.shape[0], nope_t.shape[0]
    base = start // GROUP
    whole = lambda rows, cols: pl.BlockSpec((rows, cols), lambda s: (0, 0))
    heads_of = lambda rows: pl.BlockSpec((rows, GROUP * toks), lambda s: (0, s + base))
    out = lambda rows: jax.ShapeDtypeStruct((rows, heads * toks), jnp.bfloat16)
    return pl.pallas_call(
        with_token(functools.partial(score_kernel, inv_root, which), 4),
        grid=(count // GROUP,),
        in_specs=[
            pl.BlockSpec(memory_space=pltpu.SMEM),
            pl.BlockSpec(memory_space=pltpu.SMEM),
            whole(*segments.shape),
            [whole(lat, toks)] * len(blocks),
            heads_of(lat),
            heads_of(rank),
            heads_of(value),
            heads_of(nope),
        ]
        + [pl.BlockSpec(memory_space=pl.ANY)] * len(carried),
        out_specs=[
            heads_of(span),
            heads_of(span),
            heads_of(rank),
            heads_of(lat),
        ]
        + [whole(4 * nope, rank)] * len(HOPS)
        + [TOKEN_BLOCK],
        out_shape=[
            out(span),
            out(span),
            out(rank),
            out(lat),
        ]
        + [jax.ShapeDtypeStruct((4 * nope, rank), jnp.bfloat16)] * len(HOPS)
        + [TOKEN],
        input_output_aliases={7 + len(blocks) + n: n for n in range(len(carried))},
        scratch_shapes=[
            pltpu.VMEM((4, 2, 2, nope, rank), jnp.bfloat16),
            pltpu.VMEM((span, lat), jnp.bfloat16),
            pltpu.VMEM((lat, span), jnp.bfloat16),
            pltpu.VMEM((span, toks), jnp.float32),
        ],
        compiler_params=pltpu.CompilerParams(vmem_limit_bytes=56 * MIB),
        cost_estimate=pl.CostEstimate(
            flops=8 * count * toks * span * (rank + lat),
            bytes_accessed=3 * count * 2**20,
            transcendentals=count * toks * span,
        ),
        name="score",
    )(place, block_mask, segments, blocks, qfull, dlo, dout_t, nope_t, *carried)


def key_kernel(qfull_ref, dlo_ref, probs_ref, dscore_ref, _, low_ref, total_ref):
    rank = dlo_ref.shape[0]
    step = pl.program_id(0)

    @pl.when(step == 0)
    def _():
        total_ref[...] = jnp.zeros_like(total_ref)

    total_ref[:rank] += dot_nt(qfull_ref[:rank], dscore_ref[...]) + dot_nt(dlo_ref[...], probs_ref[...])
    total_ref[rank:] += dot_nt(qfull_ref[rank:], dscore_ref[...])

    @pl.when(step == pl.num_programs(0) - 1)
    def _():
        low_ref[...] = total_ref[...].astype(low_ref.dtype)


def key_gradient(qfull, dlo, probs, dscore, toks, after):
    lat, rank, span = qfull.shape[0], dlo.shape[0], probs.shape[0]
    heads = qfull.shape[1] // toks
    heads_of = lambda rows: pl.BlockSpec((rows, GROUP * toks), lambda s: (0, s))
    return pl.pallas_call(
        with_token(key_kernel, 1),
        grid=(heads // GROUP,),
        in_specs=[heads_of(lat), heads_of(rank), heads_of(span), heads_of(span)]
        + [pl.BlockSpec(memory_space=pl.ANY)],
        out_specs=[pl.BlockSpec((lat, span), lambda s: (0, 0)), TOKEN_BLOCK],
        out_shape=[jax.ShapeDtypeStruct((lat, span), jnp.bfloat16), TOKEN],
        scratch_shapes=[pltpu.VMEM((lat, span), jnp.float32)],
        compiler_params=pltpu.CompilerParams(vmem_limit_bytes=LARGE),
        cost_estimate=pl.CostEstimate(
            flops=4 * heads * toks * span * (rank + lat), bytes_accessed=24 * MIB, transcendentals=0
        ),
        name="key_gradient",
    )(qfull, dlo, probs, dscore, after)


def split_kernel(keep_ref, got_ref, own_ref, *part_refs):
    toks = own_ref.shape[1]
    for part, part_ref in enumerate(part_refs + (own_ref,)):
        span = slice(part * toks, (part + 1) * toks)
        total = keep_ref[:, span].astype(jnp.float32) + got_ref[:, span].astype(jnp.float32)
        part_ref[...] = total.astype(part_ref.dtype)


def split(keep, got, toks):
    rows, span = keep.shape
    out = lambda dtype: jax.ShapeDtypeStruct((rows, toks), dtype)
    return pl.pallas_call(
        with_token(split_kernel),
        out_shape=[out(jnp.float32)] + [out(jnp.bfloat16)] * SPAN + [TOKEN],
        compiler_params=pltpu.CompilerParams(vmem_limit_bytes=12 * MIB),
        cost_estimate=BRIEF,
        name="split",
    )(keep, got)


def merge_kernel(own_ref, *rest):
    *part_refs, out_ref = rest
    total = own_ref[...]
    for part_ref in part_refs:
        total += part_ref[...].astype(jnp.float32)
    out_ref[...] = total.astype(out_ref.dtype)


def merge(own, parts):
    return pl.pallas_call(
        merge_kernel,
        out_shape=jax.ShapeDtypeStruct(own.shape, jnp.bfloat16),
        compiler_params=pltpu.CompilerParams(vmem_limit_bytes=12 * MIB),
        cost_estimate=BRIEF,
        name="merge",
    )(own, *parts)


def finish_kernel(own_ref, far_ref, out_ref):
    out_ref[...] = own_ref[...].astype(jnp.float32) + far_ref[...].astype(jnp.float32)


def finish(own, far):
    return pl.pallas_call(
        with_token(finish_kernel),
        out_shape=[jax.ShapeDtypeStruct(own.shape, jnp.float32), TOKEN],
        compiler_params=pltpu.CompilerParams(vmem_limit_bytes=12 * MIB),
        cost_estimate=BRIEF,
        name="finish",
    )(own, far)


def assemble_kernel(core_ref, mine_ref, other_ref, out_ref):
    rows = mine_ref.shape[0]
    core = core_ref[0]
    out_ref[pl.ds(pl.multiple_of(core * rows, rows), rows)] = mine_ref[...]
    out_ref[pl.ds(pl.multiple_of((1 - core) * rows, rows), rows)] = other_ref[...]


def assemble(core, mine, other):
    rows, toks = mine.shape
    whole = pl.BlockSpec(memory_space=pltpu.VMEM)
    return pl.pallas_call(
        with_token(assemble_kernel),
        in_specs=[pl.BlockSpec(memory_space=pltpu.SMEM), whole, whole],
        out_specs=[whole] * 2,
        out_shape=[jax.ShapeDtypeStruct((2 * rows, toks), jnp.float32), TOKEN],
        compiler_params=pltpu.CompilerParams(vmem_limit_bytes=12 * MIB),
        cost_estimate=BRIEF,
        name="assemble",
    )(core, mine, other)


def project_kernel(lout_ref, dfull_ref, wuk_ref, wuv_ref, _, att_ref, dq_ref):
    group = range(wuk_ref.shape[0])
    rank = lout_ref.shape[0]
    toks = att_ref.shape[0]
    value = wuv_ref.shape[1]
    width = dq_ref.shape[1] // len(group)
    for n in group:
        attended = dot(wuv_ref[n], lout_ref[:, n * toks : (n + 1) * toks]).astype(jnp.bfloat16)
        att_ref[:, n * value : (n + 1) * value] = attended.T
        d_full = dfull_ref[:, n * toks : (n + 1) * toks]
        d_nope = dot(wuk_ref[n], d_full[:rank]).astype(jnp.bfloat16)
        dq_ref[:, n * width : (n + 1) * width] = jnp.concatenate([d_nope, d_full[rank:]], axis=0).T


def project(lout, dfull, w_uk, w_uv, after):
    heads, nope, rank = w_uk.shape
    lat, toks = dfull.shape[0], dfull.shape[1] // heads
    value = w_uv.shape[1]
    width = nope + lat - rank
    heads_of = lambda rows, cols: pl.BlockSpec((GROUP, rows, cols), lambda s: (s, 0, 0))
    wide = lambda rows: pl.BlockSpec((rows, GROUP * toks), lambda s: (0, s))
    out = lambda cols: jax.ShapeDtypeStruct((toks, heads * cols), jnp.bfloat16)
    return pl.pallas_call(
        with_token(project_kernel),
        grid=(heads // GROUP,),
        in_specs=[wide(rank), wide(lat), heads_of(nope, rank), heads_of(value, rank)]
        + [pl.BlockSpec(memory_space=pl.ANY)],
        out_specs=[
            pl.BlockSpec((toks, GROUP * value), lambda s: (0, s)),
            pl.BlockSpec((toks, GROUP * width), lambda s: (0, s)),
            TOKEN_BLOCK,
        ],
        out_shape=[out(value), out(width), TOKEN],
        compiler_params=pltpu.CompilerParams(vmem_limit_bytes=16 * MIB),
        cost_estimate=BRIEF,
        name="project",
    )(lout, dfull, w_uk, w_uv, after)


def reduce_kernel(which, place_ref, *refs):
    *slab_refs, _, own_ref, up_ref, down_ref, far_ref = refs
    rows = own_ref.shape[0]
    for hop, out_ref in zip(HOPS, (own_ref, up_ref, down_ref, far_ref)):
        span = pl.ds(pl.multiple_of(((place_ref[which] + hop + 4) % 4) * rows, rows), rows)
        total = 0.0
        for slab_ref in slab_refs:
            total += slab_ref[span].astype(jnp.float32)
        out_ref[...] = total.astype(out_ref.dtype)


def reduced(which, place, slabs, after):
    whole = pl.BlockSpec(memory_space=pltpu.VMEM)
    rows, cols = slabs[0].shape
    return pl.pallas_call(
        with_token(functools.partial(reduce_kernel, which)),
        in_specs=[pl.BlockSpec(memory_space=pltpu.SMEM)]
        + [whole] * len(slabs)
        + [pl.BlockSpec(memory_space=pl.ANY)],
        out_specs=[whole] * 5,
        out_shape=[jax.ShapeDtypeStruct((rows // 4, cols), jnp.bfloat16)] * 4 + [TOKEN],
        compiler_params=pltpu.CompilerParams(vmem_limit_bytes=16 * MIB),
        cost_estimate=BRIEF,
        name="reduced",
    )(place, *slabs, after)


def cut_kernel(core_ref, total_ref, _, keep_ref, send_ref):
    rows = keep_ref.shape[0]
    keep_ref[...] = total_ref[pl.ds(pl.multiple_of(core_ref[0] * rows, rows), rows)]
    send_ref[...] = total_ref[pl.ds(pl.multiple_of((1 - core_ref[0]) * rows, rows), rows)]


def cut(core, total, after):
    rows, cols = total.shape
    whole = pl.BlockSpec(memory_space=pltpu.VMEM)
    return pl.pallas_call(
        cut_kernel,
        in_specs=[pl.BlockSpec(memory_space=pltpu.SMEM), whole, pl.BlockSpec(memory_space=pl.ANY)],
        out_specs=[whole] * 2,
        out_shape=[jax.ShapeDtypeStruct((rows // 2, cols), total.dtype)] * 2,
        compiler_params=pltpu.CompilerParams(vmem_limit_bytes=12 * MIB),
        cost_estimate=BRIEF,
        name="cut",
    )(core, total, after)


def total_kernel(*refs):
    *in_refs, _, out_ref = refs
    rows = in_refs[0].shape[0]
    half = len(in_refs) // 2
    for n, group in enumerate((in_refs[:half], in_refs[half:])):
        total = 0.0
        for in_ref in group:
            total += in_ref[...].astype(jnp.float32)
        out_ref[n * rows : (n + 1) * rows] = total.astype(out_ref.dtype)


def totals(first, second, after):
    whole = pl.BlockSpec(memory_space=pltpu.VMEM)
    rows, cols = first[0].shape
    return pl.pallas_call(
        total_kernel,
        in_specs=[whole] * 2 * len(first) + [pl.BlockSpec(memory_space=pl.ANY)],
        out_specs=whole,
        out_shape=jax.ShapeDtypeStruct((2 * rows, cols), jnp.bfloat16),
        compiler_params=pltpu.CompilerParams(vmem_limit_bytes=16 * MIB),
        cost_estimate=BRIEF,
        name="totals",
    )(*first, *second, after)


def pair_kernel(mine_ref, other_ref, first_ref, second_ref):
    total = mine_ref[...].astype(jnp.float32) + other_ref[...].astype(jnp.float32)
    rows = first_ref.shape[0]
    first_ref[...] = total[:rows].astype(first_ref.dtype)
    second_ref[...] = total[rows:].astype(second_ref.dtype)


def pair_up(mine, other):
    whole = pl.BlockSpec(memory_space=pltpu.VMEM)
    rows, cols = mine.shape
    return pl.pallas_call(
        pair_kernel,
        in_specs=[whole, whole],
        out_specs=[whole, whole],
        out_shape=[jax.ShapeDtypeStruct((rows // 2, cols), mine.dtype)] * 2,
        compiler_params=pltpu.CompilerParams(vmem_limit_bytes=16 * MIB),
        cost_estimate=BRIEF,
        name="pair_up",
    )(mine, other)


def stack_kernel(*refs):
    *in_refs, _, first_ref, second_ref = refs
    rows = in_refs[0].shape[0]
    half = len(in_refs) // 2
    for out_ref, group in ((first_ref, in_refs[:half]), (second_ref, in_refs[half:])):
        for n, in_ref in enumerate(group):
            out_ref[n * rows : (n + 1) * rows] = in_ref[...]


def stack(first, second, after):
    whole = pl.BlockSpec(memory_space=pltpu.VMEM)
    rows, cols = first[0].shape
    return pl.pallas_call(
        with_token(stack_kernel),
        in_specs=[whole] * 2 * len(first) + [pl.BlockSpec(memory_space=pl.ANY)],
        out_specs=[whole] * 3,
        out_shape=[jax.ShapeDtypeStruct((len(first) * rows, cols), first[0].dtype)] * 2 + [TOKEN],
        compiler_params=pltpu.CompilerParams(vmem_limit_bytes=16 * MIB),
        cost_estimate=BRIEF,
        name="stack",
    )(*first, *second, after)


def widen_kernel(chunk, place_ref, *refs):
    slab_refs = refs[: len(HOPS)]
    uk_ref, uv_ref, wide_ref, sems = refs[-4:]
    rows = slab_refs[0].shape[0] // len(HOPS)
    outer, inner = place_ref[1 + chunk], place_ref[2 - chunk]
    copies = []
    for n, slab_ref in enumerate(slab_refs):
        for m, hop in enumerate(HOPS):
            source = (inner - hop + 4) % 4
            wide_ref[n, source % 2, source // 2] = slab_ref[m * rows : (m + 1) * rows].astype(jnp.float32)
        head = 2 * (4 * chunk + (outer - HOPS[n] + 4) % 4)
        for kind, out_ref in enumerate((uk_ref, uv_ref)):
            copy = pltpu.make_async_copy(wide_ref.at[n, kind], out_ref.at[pl.ds(head, 2)], sems.at[n, kind])
            copy.start()
            copies.append(copy)
    for copy in copies:
        copy.wait()


def widen(chunk, place, slabs, heads, height, after, carried):
    cols = slabs[0].shape[1]
    somewhere = pl.BlockSpec(memory_space=pl.ANY)
    out = jax.ShapeDtypeStruct((heads, height, cols), jnp.float32)
    return pl.pallas_call(
        functools.partial(widen_kernel, chunk),
        in_specs=[pl.BlockSpec(memory_space=pltpu.SMEM)]
        + [WHOLE] * len(slabs)
        + [somewhere] * (1 + len(carried)),
        out_specs=[somewhere] * 2,
        out_shape=[out, out],
        input_output_aliases={2 + len(slabs) + n: n for n in range(len(carried))},
        scratch_shapes=[
            pltpu.VMEM((len(slabs), 2, 2, height, cols), jnp.float32),
            pltpu.SemaphoreType.DMA((len(slabs), 2)),
        ],
        compiler_params=pltpu.CompilerParams(vmem_limit_bytes=12 * MIB),
        cost_estimate=BRIEF,
        name="widen",
    )(place, *slabs, after, *carried)


def moved(block, along, back, far):
    route = []
    for x in range(4):
        for z in range(4):
            for y in range(2):
                to = ((x + along) % 4) * 8 + ((z + back) % 4) * 2 + (y + far) % 2
                route.append((x * 8 + z * 2 + y, to))
    return lax.ppermute(block, "ctx", route)


def along_x(blocks):
    return [moved(block, hop, 0, 0) for block, hop in zip(blocks, HOPS[1:])]


def along_z(blocks):
    return [moved(block, 0, hop, 0) for block, hop in zip(blocks, HOPS[1:])]


def swap_core(block):
    return lax.ppermute(block, "head", [(0, 1), (1, 0), (2, 3), (3, 2)])


def swap_far(block):
    return lax.ppermute(block, "head", [(0, 2), (2, 0), (1, 3), (3, 1)])


def body(latent, query, d_out, w_uk, w_uv, block_mask, segments):
    toks, lat = latent.shape
    heads, nope, rank = w_uk.shape
    width = query.shape[1] // heads
    inv_root = 1.0 / math.sqrt(width)
    position = lax.axis_index("ctx")
    seg_rows = segments.reshape(-1, toks)
    latent_t = latent.T
    blocks = [shifted(latent_t, "ctx", distance) for distance in (2, 1)] + [latent_t]
    qfull, dlo, dout_t, nope_t = prepare(query, d_out, w_uk, w_uv)

    core = (lax.axis_index("head") % 2).astype(jnp.int32).reshape(1)
    carried = []
    slabs = []
    count = heads // CHUNKS
    place = jnp.stack([position, position // 8, position // 2 % 4]).astype(jnp.int32)
    for chunk in range(CHUNKS):
        outputs = score(
            1 + chunk,
            place,
            block_mask,
            seg_rows,
            blocks,
            qfull,
            dlo,
            dout_t,
            nope_t,
            inv_root,
            chunk * count,
            count,
            carried,
        )
        carried = outputs[:4]
        slabs.append(outputs[4:8])
        token = outputs[8]
    probs, dscore, lout, dfull = carried
    first, second = slabs
    *first, token = reduced(2, place, [first[0]] + along_x(first[1:]), token)
    total, token = key_gradient(qfull, dlo, probs, dscore, toks, token)
    *second, token = reduced(1, place, [second[0]] + along_z(second[1:]), token)
    keep, send = cut(core, total, token)
    own, *parts, token = split(keep, swap_core(send), toks)
    mine = totals([first[0]] + along_z(first[1:]), [second[0]] + along_x(second[1:]), token)
    low = merge(own, [shifted(parts[part], "ctx", part - SPAN) for part in range(SPAN)])
    first, second = pair_up(mine, moved(mine, 0, 0, 1))
    half, token = finish(low, swap_far(low))
    d_latent_t, token = assemble(core, half, swap_core(half))
    first, second, token = stack([first] + along_z([first] * 3), [second] + along_x([second] * 3), token)
    attended, d_query, token = project(lout, dfull, w_uk, w_uv, token)
    grads = widen(0, place, [first] + along_x([first] * 3), heads, nope, token, [])
    d_w_uk, d_w_uv = widen(1, place, [second] + along_z([second] * 3), heads, nope, token, grads)
    return attended, d_query, d_latent_t.T, d_w_uk, d_w_uv


def solution(mesh):
    in_specs = (
        P("ctx", None),
        P("ctx", "head"),
        P("ctx", "head"),
        P("head", None, None),
        P("head", None, None),
        P(),
        P(),
    )
    out_specs = (
        P("ctx", "head"),
        P("ctx", "head"),
        P("ctx", None),
        P("head", None, None),
        P("head", None, None),
    )
    return jax.shard_map(body, mesh=mesh, in_specs=in_specs, out_specs=out_specs, check_vma=False)
```

```python
import functools
import math

import jax
import jax.numpy as jnp
from jax import lax
from jax.experimental import pallas as pl
from jax.experimental.pallas import tpu as pltpu
from jax.sharding import PartitionSpec as P

SPAN = 2
CHUNKS = 2
HOPS = (0, 1, -1, 2)
GROUP = 4
LOG2E = 1.4426950408889634
MIB = 2**20
LARGE = 56 * MIB
BRIEF = pl.CostEstimate(flops=2**20, bytes_accessed=2**20, transcendentals=0)


def shifted(block, axis, distance):
    devices = range(lax.axis_size(axis))
    route = [(i - distance, i) for i in devices if i - distance in devices]
    return lax.ppermute(block, axis, route)

TOKEN = jax.ShapeDtypeStruct((8, 128), jnp.float32)
WHOLE = pl.BlockSpec(memory_space=pltpu.VMEM)
TOKEN_BLOCK = pl.BlockSpec(memory_space=pltpu.HBM)


def with_token(kernel, scratch=0):
    def wrapped(*refs):
        end = len(refs) - scratch
        kernel(*refs[: end - 1], *refs[end:])

    return wrapped


def dot(a, b):
    return lax.dot_general(a, b, (((1,), (0,)), ((), ())), preferred_element_type=jnp.float32)


def dot_nt(a, b):
    return lax.dot_general(a, b, (((1,), (1,)), ((), ())), preferred_element_type=jnp.float32)


def prepare_kernel(query_ref, dout_ref, wuk_ref, wuv_ref, qfull_ref, dlo_ref, dout_t_ref, nope_t_ref):
    nope = wuk_ref.shape[1]
    value = wuv_ref.shape[1]
    width = query_ref.shape[1] // wuk_ref.shape[0]
    rank = wuk_ref.shape[2]
    toks = query_ref.shape[0]
    query_t = query_ref[...].T
    dout_t = dout_ref[...].T
    for n in range(wuk_ref.shape[0]):
        q_nope = query_t[n * width : n * width + nope]
        grads = dout_t[n * value : (n + 1) * value]
        span = slice(n * toks, (n + 1) * toks)
        nope_t_ref[:, span] = q_nope
        dout_t_ref[:, span] = grads
        qfull_ref[:rank, span] = dot(wuk_ref[n].T, q_nope).astype(jnp.bfloat16)
        qfull_ref[rank:, span] = query_t[n * width + nope : (n + 1) * width]
        dlo_ref[:, span] = dot(wuv_ref[n].T, grads).astype(jnp.bfloat16)


def prepare(query, d_out, w_uk, w_uv):
    toks = query.shape[0]
    heads, nope, rank = w_uk.shape
    value = w_uv.shape[1]
    width = query.shape[1] // heads
    lat = rank + width - nope
    shape = lambda rows: jax.ShapeDtypeStruct((rows, heads * toks), jnp.bfloat16)
    block = lambda rows: pl.BlockSpec((rows, GROUP * toks), lambda s: (0, s))
    return pl.pallas_call(
        prepare_kernel,
        grid=(heads // GROUP,),
        in_specs=[
            pl.BlockSpec((toks, GROUP * width), lambda s: (0, s)),
            pl.BlockSpec((toks, GROUP * value), lambda s: (0, s)),
            pl.BlockSpec((GROUP, nope, rank), lambda s: (s, 0, 0)),
            pl.BlockSpec((GROUP, value, rank), lambda s: (s, 0, 0)),
        ],
        out_specs=[block(lat), block(rank), block(value), block(nope)],
        out_shape=[shape(lat), shape(rank), shape(value), shape(nope)],
        compiler_params=pltpu.CompilerParams(vmem_limit_bytes=LARGE),
        cost_estimate=pl.CostEstimate(
            flops=4 * heads * toks * nope * rank, bytes_accessed=16 * 2**20, transcendentals=0
        ),
        name="prepare",
    )(query, d_out, w_uk, w_uv)


def score_kernel(
    inv_root,
    which,
    place_ref,
    mask_ref,
    segments_ref,
    block_refs,
    qfull_ref,
    dlo_ref,
    dout_t_ref,
    nope_t_ref,
    *rest,
):
    probs_ref, dscore_ref, lout_ref, dfull_ref, *slab_refs, grad_ref, keys_ref, keys_t_ref, bias_ref = rest[-12:]
    rank = dlo_ref.shape[0]
    toks = block_refs[0].shape[1]
    group = range(qfull_ref.shape[1] // toks)
    step = pl.program_id(0)

    @pl.when(step == 0)
    def _():
        for n, block_ref in enumerate(block_refs):
            keys_t_ref[:, n * toks : (n + 1) * toks] = block_ref[...]
            keys_ref[n * toks : (n + 1) * toks] = block_ref[...].T
        position = place_ref[0]
        seg_query = segments_ref[:, pl.ds(pl.multiple_of(position * toks, toks), toks)].astype(jnp.float32)
        for n in range(len(block_refs)):
            distance = len(block_refs) - 1 - n
            block = jnp.maximum(position - distance, 0)
            seg_row = segments_ref[:, pl.ds(pl.multiple_of(block * toks, toks), toks)].astype(jnp.float32)
            seg_key = jnp.broadcast_to(seg_row, (toks, toks)).T
            granted = jnp.broadcast_to(mask_ref[position, block], (toks, toks)) == 1
            allowed = (seg_key == seg_query) | granted
            if distance == 0:
                key, query = (lax.broadcasted_iota(jnp.int32, (toks, toks), axis) for axis in (0, 1))
                allowed &= key <= query
            else:
                allowed &= jnp.broadcast_to(position, (toks, toks)) >= distance
            bias_ref[n * toks : (n + 1) * toks] = jnp.where(allowed, 0.0, -jnp.inf)

    def slab(n):
        return (step * (len(group) // 2) + n // 2 + 4 - place_ref[which]) % 4

    part = lambda ref, n: ref[:, n * toks : (n + 1) * toks]
    scores = dot(keys_ref[...], qfull_ref[...])
    probs = []
    for n in group:
        scaled = scores[:, n * toks : (n + 1) * toks] * (inv_root * LOG2E) + bias_ref[...]
        weights = jnp.exp2(scaled - jnp.max(scaled, axis=0, keepdims=True))
        probs.append(weights * (1.0 / jnp.sum(weights, axis=0, keepdims=True)))
        probs_ref[:, n * toks : (n + 1) * toks] = probs[n].astype(jnp.bfloat16)
    d_probs = dot(keys_ref[:, :rank], dlo_ref[...])
    lout_ref[...] = dot(keys_t_ref[:rank], probs_ref[...]).astype(jnp.bfloat16)
    for n in group:
        d_prob = d_probs[:, n * toks : (n + 1) * toks]
        delta = jnp.sum(probs[n] * d_prob, axis=0, keepdims=True)
        d_score = probs[n] * (d_prob - delta) * inv_root
        dscore_ref[:, n * toks : (n + 1) * toks] = d_score.astype(jnp.bfloat16)
    for n in group:
        grad_ref[slab(n), n % 2, 1] = dot_nt(part(dout_t_ref, n), part(lout_ref, n)).astype(jnp.bfloat16)
    dfull_ref[...] = dot(keys_t_ref[...], dscore_ref[...]).astype(jnp.bfloat16)
    for n in group:
        d_absorbed = dfull_ref[:rank, n * toks : (n + 1) * toks]
        grad_ref[slab(n), n % 2, 0] = dot_nt(part(nope_t_ref, n), d_absorbed).astype(jnp.bfloat16)

    @pl.when(step == pl.num_programs(0) - 1)
    def _():
        for hop, slab_ref in zip(HOPS, slab_refs):
            slab_ref[...] = grad_ref[hop % 4].reshape(slab_ref.shape)


def score(which, place, block_mask, segments, blocks, qfull, dlo, dout_t, nope_t, inv_root, start, count, carried):
    lat, toks = blocks[0].shape
    heads = qfull.shape[1] // toks
    span = len(blocks) * toks
    rank = dlo.shape[0]
    value, nope = dout_t.shape[0], nope_t.shape[0]
    base = start // GROUP
    whole = lambda rows, cols: pl.BlockSpec((rows, cols), lambda s: (0, 0))
    heads_of = lambda rows: pl.BlockSpec((rows, GROUP * toks), lambda s: (0, s + base))
    out = lambda rows: jax.ShapeDtypeStruct((rows, heads * toks), jnp.bfloat16)
    return pl.pallas_call(
        with_token(functools.partial(score_kernel, inv_root, which), 4),
        grid=(count // GROUP,),
        in_specs=[
            pl.BlockSpec(memory_space=pltpu.SMEM),
            pl.BlockSpec(memory_space=pltpu.SMEM),
            whole(*segments.shape),
            [whole(lat, toks)] * len(blocks),
            heads_of(lat),
            heads_of(rank),
            heads_of(value),
            heads_of(nope),
        ]
        + [pl.BlockSpec(memory_space=pl.ANY)] * len(carried),
        out_specs=[
            heads_of(span),
            heads_of(span),
            heads_of(rank),
            heads_of(lat),
        ]
        + [whole(4 * nope, rank)] * len(HOPS)
        + [TOKEN_BLOCK],
        out_shape=[
            out(span),
            out(span),
            out(rank),
            out(lat),
        ]
        + [jax.ShapeDtypeStruct((4 * nope, rank), jnp.bfloat16)] * len(HOPS)
        + [TOKEN],
        input_output_aliases={7 + len(blocks) + n: n for n in range(len(carried))},
        scratch_shapes=[
            pltpu.VMEM((4, 2, 2, nope, rank), jnp.bfloat16),
            pltpu.VMEM((span, lat), jnp.bfloat16),
            pltpu.VMEM((lat, span), jnp.bfloat16),
            pltpu.VMEM((span, toks), jnp.float32),
        ],
        compiler_params=pltpu.CompilerParams(vmem_limit_bytes=56 * MIB),
        cost_estimate=pl.CostEstimate(
            flops=8 * count * toks * span * (rank + lat),
            bytes_accessed=3 * count * 2**20,
            transcendentals=count * toks * span,
        ),
        name="score",
    )(place, block_mask, segments, blocks, qfull, dlo, dout_t, nope_t, *carried)


def key_kernel(qfull_ref, dlo_ref, probs_ref, dscore_ref, _, low_ref, total_ref):
    rank = dlo_ref.shape[0]
    step = pl.program_id(0)

    @pl.when(step == 0)
    def _():
        total_ref[...] = jnp.zeros_like(total_ref)

    total_ref[:rank] += dot_nt(qfull_ref[:rank], dscore_ref[...]) + dot_nt(dlo_ref[...], probs_ref[...])
    total_ref[rank:] += dot_nt(qfull_ref[rank:], dscore_ref[...])

    @pl.when(step == pl.num_programs(0) - 1)
    def _():
        low_ref[...] = total_ref[...].astype(low_ref.dtype)


def key_gradient(qfull, dlo, probs, dscore, toks, after):
    lat, rank, span = qfull.shape[0], dlo.shape[0], probs.shape[0]
    heads = qfull.shape[1] // toks
    heads_of = lambda rows: pl.BlockSpec((rows, GROUP * toks), lambda s: (0, s))
    return pl.pallas_call(
        with_token(key_kernel, 1),
        grid=(heads // GROUP,),
        in_specs=[heads_of(lat), heads_of(rank), heads_of(span), heads_of(span)]
        + [pl.BlockSpec(memory_space=pl.ANY)],
        out_specs=[pl.BlockSpec((lat, span), lambda s: (0, 0)), TOKEN_BLOCK],
        out_shape=[jax.ShapeDtypeStruct((lat, span), jnp.bfloat16), TOKEN],
        scratch_shapes=[pltpu.VMEM((lat, span), jnp.float32)],
        compiler_params=pltpu.CompilerParams(vmem_limit_bytes=LARGE),
        cost_estimate=pl.CostEstimate(
            flops=4 * heads * toks * span * (rank + lat), bytes_accessed=24 * MIB, transcendentals=0
        ),
        name="key_gradient",
    )(qfull, dlo, probs, dscore, after)


def split_kernel(keep_ref, got_ref, own_ref, *part_refs):
    toks = own_ref.shape[1]
    for part, part_ref in enumerate(part_refs + (own_ref,)):
        span = slice(part * toks, (part + 1) * toks)
        total = keep_ref[:, span].astype(jnp.float32) + got_ref[:, span].astype(jnp.float32)
        part_ref[...] = total.astype(part_ref.dtype)


def split(keep, got, toks):
    rows, span = keep.shape
    out = lambda dtype: jax.ShapeDtypeStruct((rows, toks), dtype)
    return pl.pallas_call(
        with_token(split_kernel),
        out_shape=[out(jnp.float32)] + [out(jnp.bfloat16)] * SPAN + [TOKEN],
        compiler_params=pltpu.CompilerParams(vmem_limit_bytes=12 * MIB),
        cost_estimate=BRIEF,
        name="split",
    )(keep, got)


def merge_kernel(own_ref, *rest):
    *part_refs, out_ref = rest
    total = own_ref[...]
    for part_ref in part_refs:
        total += part_ref[...].astype(jnp.float32)
    out_ref[...] = total.astype(out_ref.dtype)


def merge(own, parts):
    return pl.pallas_call(
        merge_kernel,
        out_shape=jax.ShapeDtypeStruct(own.shape, jnp.bfloat16),
        compiler_params=pltpu.CompilerParams(vmem_limit_bytes=12 * MIB),
        cost_estimate=BRIEF,
        name="merge",
    )(own, *parts)


def finish_kernel(own_ref, far_ref, out_ref):
    out_ref[...] = own_ref[...].astype(jnp.float32) + far_ref[...].astype(jnp.float32)


def finish(own, far):
    return pl.pallas_call(
        with_token(finish_kernel),
        out_shape=[jax.ShapeDtypeStruct(own.shape, jnp.float32), TOKEN],
        compiler_params=pltpu.CompilerParams(vmem_limit_bytes=12 * MIB),
        cost_estimate=BRIEF,
        name="finish",
    )(own, far)


def assemble_kernel(core_ref, mine_ref, other_ref, out_ref):
    rows = mine_ref.shape[0]
    core = core_ref[0]
    out_ref[pl.ds(pl.multiple_of(core * rows, rows), rows)] = mine_ref[...]
    out_ref[pl.ds(pl.multiple_of((1 - core) * rows, rows), rows)] = other_ref[...]


def assemble(core, mine, other):
    rows, toks = mine.shape
    whole = pl.BlockSpec(memory_space=pltpu.VMEM)
    return pl.pallas_call(
        with_token(assemble_kernel),
        in_specs=[pl.BlockSpec(memory_space=pltpu.SMEM), whole, whole],
        out_specs=[whole] * 2,
        out_shape=[jax.ShapeDtypeStruct((2 * rows, toks), jnp.float32), TOKEN],
        compiler_params=pltpu.CompilerParams(vmem_limit_bytes=12 * MIB),
        cost_estimate=BRIEF,
        name="assemble",
    )(core, mine, other)


def project_kernel(lout_ref, dfull_ref, wuk_ref, wuv_ref, _, att_ref, dq_ref):
    group = range(wuk_ref.shape[0])
    rank = lout_ref.shape[0]
    toks = att_ref.shape[0]
    value = wuv_ref.shape[1]
    width = dq_ref.shape[1] // len(group)
    for n in group:
        attended = dot(wuv_ref[n], lout_ref[:, n * toks : (n + 1) * toks]).astype(jnp.bfloat16)
        att_ref[:, n * value : (n + 1) * value] = attended.T
        d_full = dfull_ref[:, n * toks : (n + 1) * toks]
        d_nope = dot(wuk_ref[n], d_full[:rank]).astype(jnp.bfloat16)
        dq_ref[:, n * width : (n + 1) * width] = jnp.concatenate([d_nope, d_full[rank:]], axis=0).T


def project(lout, dfull, w_uk, w_uv, after):
    heads, nope, rank = w_uk.shape
    lat, toks = dfull.shape[0], dfull.shape[1] // heads
    value = w_uv.shape[1]
    width = nope + lat - rank
    heads_of = lambda rows, cols: pl.BlockSpec((GROUP, rows, cols), lambda s: (s, 0, 0))
    wide = lambda rows: pl.BlockSpec((rows, GROUP * toks), lambda s: (0, s))
    out = lambda cols: jax.ShapeDtypeStruct((toks, heads * cols), jnp.bfloat16)
    return pl.pallas_call(
        with_token(project_kernel),
        grid=(heads // GROUP,),
        in_specs=[wide(rank), wide(lat), heads_of(nope, rank), heads_of(value, rank)]
        + [pl.BlockSpec(memory_space=pl.ANY)],
        out_specs=[
            pl.BlockSpec((toks, GROUP * value), lambda s: (0, s)),
            pl.BlockSpec((toks, GROUP * width), lambda s: (0, s)),
            TOKEN_BLOCK,
        ],
        out_shape=[out(value), out(width), TOKEN],
        compiler_params=pltpu.CompilerParams(vmem_limit_bytes=16 * MIB),
        cost_estimate=BRIEF,
        name="project",
    )(lout, dfull, w_uk, w_uv, after)


def reduce_kernel(which, place_ref, *refs):
    *slab_refs, _, own_ref, up_ref, down_ref, far_ref = refs
    rows = own_ref.shape[0]
    for hop, out_ref in zip(HOPS, (own_ref, up_ref, down_ref, far_ref)):
        span = pl.ds(pl.multiple_of(((place_ref[which] + hop + 4) % 4) * rows, rows), rows)
        total = 0.0
        for slab_ref in slab_refs:
            total += slab_ref[span].astype(jnp.float32)
        out_ref[...] = total.astype(out_ref.dtype)


def reduced(which, place, slabs, after):
    whole = pl.BlockSpec(memory_space=pltpu.VMEM)
    rows, cols = slabs[0].shape
    return pl.pallas_call(
        with_token(functools.partial(reduce_kernel, which)),
        in_specs=[pl.BlockSpec(memory_space=pltpu.SMEM)]
        + [whole] * len(slabs)
        + [pl.BlockSpec(memory_space=pl.ANY)],
        out_specs=[whole] * 4 + [TOKEN_BLOCK],
        out_shape=[jax.ShapeDtypeStruct((rows // 4, cols), jnp.bfloat16)] * 4 + [TOKEN],
        compiler_params=pltpu.CompilerParams(vmem_limit_bytes=16 * MIB),
        cost_estimate=BRIEF,
        name="reduced",
    )(place, *slabs, after)


def cut_kernel(core_ref, total_ref, _, keep_ref, send_ref):
    rows = keep_ref.shape[0]
    keep_ref[...] = total_ref[pl.ds(pl.multiple_of(core_ref[0] * rows, rows), rows)]
    send_ref[...] = total_ref[pl.ds(pl.multiple_of((1 - core_ref[0]) * rows, rows), rows)]


def cut(core, total, after):
    rows, cols = total.shape
    whole = pl.BlockSpec(memory_space=pltpu.VMEM)
    return pl.pallas_call(
        cut_kernel,
        in_specs=[pl.BlockSpec(memory_space=pltpu.SMEM), whole, pl.BlockSpec(memory_space=pl.ANY)],
        out_specs=[whole] * 2,
        out_shape=[jax.ShapeDtypeStruct((rows // 2, cols), total.dtype)] * 2,
        compiler_params=pltpu.CompilerParams(vmem_limit_bytes=12 * MIB),
        cost_estimate=BRIEF,
        name="cut",
    )(core, total, after)


def total_kernel(*refs):
    *in_refs, _, out_ref = refs
    rows = in_refs[0].shape[0]
    half = len(in_refs) // 2
    for n, group in enumerate((in_refs[:half], in_refs[half:])):
        total = 0.0
        for in_ref in group:
            total += in_ref[...].astype(jnp.float32)
        out_ref[n * rows : (n + 1) * rows] = total.astype(out_ref.dtype)


def totals(first, second, after):
    whole = pl.BlockSpec(memory_space=pltpu.VMEM)
    rows, cols = first[0].shape
    return pl.pallas_call(
        total_kernel,
        in_specs=[whole] * 2 * len(first) + [pl.BlockSpec(memory_space=pl.ANY)],
        out_specs=whole,
        out_shape=jax.ShapeDtypeStruct((2 * rows, cols), jnp.bfloat16),
        compiler_params=pltpu.CompilerParams(vmem_limit_bytes=16 * MIB),
        cost_estimate=BRIEF,
        name="totals",
    )(*first, *second, after)


def pair_kernel(mine_ref, other_ref, first_ref, second_ref):
    total = mine_ref[...].astype(jnp.float32) + other_ref[...].astype(jnp.float32)
    rows = first_ref.shape[0]
    first_ref[...] = total[:rows].astype(first_ref.dtype)
    second_ref[...] = total[rows:].astype(second_ref.dtype)


def pair_up(mine, other):
    whole = pl.BlockSpec(memory_space=pltpu.VMEM)
    rows, cols = mine.shape
    return pl.pallas_call(
        pair_kernel,
        in_specs=[whole, whole],
        out_specs=[whole, whole],
        out_shape=[jax.ShapeDtypeStruct((rows // 2, cols), mine.dtype)] * 2,
        compiler_params=pltpu.CompilerParams(vmem_limit_bytes=16 * MIB),
        cost_estimate=BRIEF,
        name="pair_up",
    )(mine, other)


def stack_kernel(*refs):
    *in_refs, _, first_ref, second_ref = refs
    rows = in_refs[0].shape[0]
    half = len(in_refs) // 2
    for out_ref, group in ((first_ref, in_refs[:half]), (second_ref, in_refs[half:])):
        for n, in_ref in enumerate(group):
            out_ref[n * rows : (n + 1) * rows] = in_ref[...]


def stack(first, second, after):
    whole = pl.BlockSpec(memory_space=pltpu.VMEM)
    rows, cols = first[0].shape
    return pl.pallas_call(
        with_token(stack_kernel),
        in_specs=[whole] * 2 * len(first) + [pl.BlockSpec(memory_space=pl.ANY)],
        out_specs=[whole] * 2 + [TOKEN_BLOCK],
        out_shape=[jax.ShapeDtypeStruct((len(first) * rows, cols), first[0].dtype)] * 2 + [TOKEN],
        compiler_params=pltpu.CompilerParams(vmem_limit_bytes=16 * MIB),
        cost_estimate=BRIEF,
        name="stack",
    )(*first, *second, after)


def widen_kernel(chunk, place_ref, *refs):
    slab_refs = refs[: len(HOPS)]
    uk_ref, uv_ref, wide_ref, sems = refs[-4:]
    rows = slab_refs[0].shape[0] // len(HOPS)
    outer, inner = place_ref[1 + chunk], place_ref[2 - chunk]
    copies = []
    for n, slab_ref in enumerate(slab_refs):
        for m, hop in enumerate(HOPS):
            source = (inner - hop + 4) % 4
            wide_ref[n, source % 2, source // 2] = slab_ref[m * rows : (m + 1) * rows].astype(jnp.float32)
        head = 2 * (4 * chunk + (outer - HOPS[n] + 4) % 4)
        for kind, out_ref in enumerate((uk_ref, uv_ref)):
            copy = pltpu.make_async_copy(wide_ref.at[n, kind], out_ref.at[pl.ds(head, 2)], sems.at[n, kind])
            copy.start()
            copies.append(copy)
    for copy in copies:
        copy.wait()


def widen(chunk, place, slabs, heads, height, after, carried):
    cols = slabs[0].shape[1]
    somewhere = pl.BlockSpec(memory_space=pl.ANY)
    out = jax.ShapeDtypeStruct((heads, height, cols), jnp.float32)
    return pl.pallas_call(
        functools.partial(widen_kernel, chunk),
        in_specs=[pl.BlockSpec(memory_space=pltpu.SMEM)]
        + [WHOLE] * len(slabs)
        + [somewhere] * (1 + len(carried)),
        out_specs=[somewhere] * 2,
        out_shape=[out, out],
        input_output_aliases={2 + len(slabs) + n: n for n in range(len(carried))},
        scratch_shapes=[
            pltpu.VMEM((len(slabs), 2, 2, height, cols), jnp.float32),
            pltpu.SemaphoreType.DMA((len(slabs), 2)),
        ],
        compiler_params=pltpu.CompilerParams(vmem_limit_bytes=12 * MIB),
        cost_estimate=BRIEF,
        name="widen",
    )(place, *slabs, after, *carried)


def moved(block, along, back, far):
    route = []
    for x in range(4):
        for z in range(4):
            for y in range(2):
                to = ((x + along) % 4) * 8 + ((z + back) % 4) * 2 + (y + far) % 2
                route.append((x * 8 + z * 2 + y, to))
    return lax.ppermute(block, "ctx", route)


def along_x(blocks):
    return [moved(block, hop, 0, 0) for block, hop in zip(blocks, HOPS[1:])]


def along_z(blocks):
    return [moved(block, 0, hop, 0) for block, hop in zip(blocks, HOPS[1:])]


def swap_core(block):
    return lax.ppermute(block, "head", [(0, 1), (1, 0), (2, 3), (3, 2)])


def swap_far(block):
    return lax.ppermute(block, "head", [(0, 2), (2, 0), (1, 3), (3, 1)])


def body(latent, query, d_out, w_uk, w_uv, block_mask, segments):
    toks, lat = latent.shape
    heads, nope, rank = w_uk.shape
    width = query.shape[1] // heads
    inv_root = 1.0 / math.sqrt(width)
    position = lax.axis_index("ctx")
    seg_rows = segments.reshape(1, -1)
    latent_t = latent.T
    blocks = [shifted(latent_t, "ctx", distance) for distance in (2, 1)] + [latent_t]
    qfull, dlo, dout_t, nope_t = prepare(query, d_out, w_uk, w_uv)

    core = (lax.axis_index("head") % 2).astype(jnp.int32).reshape(1)
    carried = []
    slabs = []
    count = heads // CHUNKS
    place = jnp.stack([position, position // 8, position // 2 % 4]).astype(jnp.int32)
    for chunk in range(CHUNKS):
        outputs = score(
            1 + chunk,
            place,
            block_mask,
            seg_rows,
            blocks,
            qfull,
            dlo,
            dout_t,
            nope_t,
            inv_root,
            chunk * count,
            count,
            carried,
        )
        carried = outputs[:4]
        slabs.append(outputs[4:8])
        token = outputs[8]
    probs, dscore, lout, dfull = carried
    first, second = slabs
    *first, token = reduced(2, place, [first[0]] + along_x(first[1:]), token)
    total, token = key_gradient(qfull, dlo, probs, dscore, toks, token)
    *second, token = reduced(1, place, [second[0]] + along_z(second[1:]), token)
    keep, send = cut(core, total, token)
    own, *parts, token = split(keep, swap_core(send), toks)
    mine = totals([first[0]] + along_z(first[1:]), [second[0]] + along_x(second[1:]), token)
    low = merge(own, [shifted(parts[part], "ctx", part - SPAN) for part in range(SPAN)])
    first, second = pair_up(mine, moved(mine, 0, 0, 1))
    half, token = finish(low, swap_far(low))
    d_latent_t, token = assemble(core, half, swap_core(half))
    first, second, token = stack([first] + along_z([first] * 3), [second] + along_x([second] * 3), token)
    attended, d_query, token = project(lout, dfull, w_uk, w_uv, token)
    grads = widen(0, place, [first] + along_x([first] * 3), heads, nope, token, [])
    d_w_uk, d_w_uv = widen(1, place, [second] + along_z([second] * 3), heads, nope, token, grads)
    return attended, d_query, d_latent_t.T, d_w_uk, d_w_uv


def solution(mesh):
    in_specs = (
        P("ctx", None),
        P("ctx", "head"),
        P("ctx", "head"),
        P("head", None, None),
        P("head", None, None),
        P(),
        P(),
    )
    out_specs = (
        P("ctx", "head"),
        P("ctx", "head"),
        P("ctx", None),
        P("head", None, None),
        P("head", None, None),
    )
    return jax.shard_map(body, mesh=mesh, in_specs=in_specs, out_specs=out_specs, check_vma=False)
```
